32 devices in a mesh: groups: 2 (over y), rows: 4 (over z), section: 4 (over x, core).
Axes of the slice: x: 2, y: 2, z: 4, core: 2. Of those that a mesh axis runs over, the one named last changes fastest.
Arguments:
- latent: bfloat16 [8, 16, 16, 768], P('groups', 'rows'), parts along dimension 0, may hold values from -1000 to 1000
- target: bfloat16 [8, 16, 16, 768], P('groups', 'rows'), parts along dimension 0, may hold values from -60 to 60
- expand_weight: bfloat16 [4, 768, 1536], P('section', 'rows'), may hold values from -0.21875 to 0.21875
- expand_bias: float32 [4, 1536], P('section'), may hold values from -2 to 2
- reduce_weight: bfloat16 [4, 1536, 768], P('section', 'rows'), may hold values from -0.15625 to 0.15625
- reduce_bias: float32 [4, 768], P('section'), may hold values from -2 to 2
- depth_kernel: float32 [4, 49, 768], P('section'), may hold values from -0.8 to 0.8
- depth_offset: float32 [4, 768], P('section'), may hold values from -2 to 2
- norm_gain: float32 [4, 768], P('section'), may hold values from 0.1 to 1.9
- norm_shift: float32 [4, 768], P('section'), may hold values from -1.2 to 1.2
- layer_scale: float32 [4, 768], P('section'), may hold values from 0.2 to 0.6
Outputs:
- kernel_gradient: float32 [8, 49, 768], P(('groups', 'section')), parts along dimension 0
- offset_gradient: float32 [8, 768], P(('groups', 'section')), parts along dimension 0
- gain_gradient: float32 [8, 768], P(('groups', 'section')), parts along dimension 0
- shift_gradient: float32 [8, 768], P(('groups', 'section')), parts along dimension 0
- scale_gradient: float32 [8, 768], P(('groups', 'section')), parts along dimension 0
The draws below stay inside these ranges and needn't reach their ends.
There are 2 independent parts, one for each index of `groups`. The reference program is written for one: setup_inputs(seed, part) draws one part's arguments, and reference() takes and returns one part's arrays. A program takes and returns all parts, laid end to end along the dimension named above; an argument that names none is the same for every part. Nothing has to cross between parts.
All inputs are finite; a program needn't handle non-finite values.
Results may differ from the reference program's by a relative error of at most 0.005.
The reference program's roundings to bfloat16 on the way count: a program that leaves them out, or rounds other values in their place, can miss the bound.
Values may be sent and summed in bfloat16 or wider, within the bound.
A program may use at most 64 MiB of HBM per device.

```python
import math
import jax
import jax.numpy as jnp
from jax import lax

D = 768
FF = 1536
KS = 7
MB = 4
COLS = 16
H = 16
BLOCKS = 4


def draw_latent(key, part):
    key_base, key_rows, key_chan = jax.random.split(key, 3)
    position = jnp.arange(H, dtype=jnp.float32) / max(H - 1, 1)
    rise = 1.0 + 2.0 * position
    base = jnp.clip(jax.random.normal(key_base, (MB, H, COLS, D), jnp.float32), -6.0, 6.0)
    token_scale = jnp.exp(jax.random.uniform(key_rows, (MB, H, COLS, 1), jnp.float32, 0.0, math.log(10.0)))
    channel_scale = jnp.exp(jax.random.uniform(key_chan, (D,), jnp.float32, math.log(0.3), math.log(3.0)))
    values = base * token_scale * channel_scale * rise[None, :, None, None]
    return values.astype(jnp.bfloat16)


def draw_target(key, part):
    key_base = jax.random.fold_in(jax.random.fold_in(key, 7), 0)
    position = jnp.arange(H, dtype=jnp.float32) / max(H - 1, 1)
    rise = 1.0 + 2.0 * position
    base = jnp.clip(jax.random.normal(key_base, (MB, H, COLS, D), jnp.float32), -6.0, 6.0)
    values = 3.0 * base * rise[None, :, None, None]
    return values.astype(jnp.bfloat16)


def steps_of(own_key, extent, shards, smallest, high):
    def one(axis_at, parts):
        draws = jax.random.uniform(jax.random.fold_in(jax.random.fold_in(own_key, 6), axis_at), (parts,), jnp.float32, smallest / len(shards), high / len(shards))
        return jnp.repeat(jnp.exp(draws), extent[axis_at] // parts).reshape((-1,) + (1,) * (len(extent) - axis_at - 1))

    factor_of = one(*shards[0])
    for cut in shards[1:]:
        factor_of = factor_of * one(*cut)
    return factor_of


def noise(key, shape, deviation, limit, cuts=(), held_as=jnp.bfloat16):
    factor_of = steps_of(key, shape, cuts, -0.22, 0.18) if cuts else 1.0
    values = jax.random.normal(key, shape, jnp.float32) * deviation * factor_of
    return jnp.minimum(jnp.maximum(values, -limit), limit).astype(held_as)


def setup_inputs(seed: int = 0, part: int = 0) -> dict:
    keys = jax.random.split(jax.random.key(seed), 12)
    part_splits = jax.random.split(jax.random.fold_in(keys[11], part), 12)
    latent = draw_latent(jax.random.fold_in(jax.random.fold_in(keys[11], part), 71), part)
    target = draw_target(jax.random.fold_in(jax.random.fold_in(keys[11], part), 71), part)
    expand_weight = noise(keys[2], (BLOCKS, D, FF), D ** -0.5, 0.21875, ((0, 4), (1, 4)))
    expand_bias = noise(keys[3], (BLOCKS, FF), 0.5, 2.0, ((0, 4),), jnp.float32)
    reduce_weight = noise(keys[4], (BLOCKS, FF, D), FF ** -0.5, 0.15625, ((0, 4), (1, 4)))
    reduce_bias = noise(keys[5], (BLOCKS, D), 0.5, 2.0, ((0, 4),), jnp.float32)
    depth_kernel = noise(keys[6], (BLOCKS, KS * KS, D), 0.2, 0.8, ((0, 4),), jnp.float32)
    depth_offset = noise(keys[7], (BLOCKS, D), 0.5, 2.0, ((0, 4),), jnp.float32)
    norm_gain = jnp.clip(1.0 + 0.18 * jax.random.normal(keys[8], (BLOCKS, D), jnp.float32), 0.1, 1.9)
    norm_shift = noise(keys[9], (BLOCKS, D), 0.3, 1.2, ((0, 4),), jnp.float32)
    layer_scale = jnp.clip(0.2 + 0.400000021 * jax.random.uniform(keys[10], (BLOCKS, D), jnp.float32) ** steps_of(keys[10], (BLOCKS, D), ((0, 4),), -0.2, 0.2), 0.2, 0.6)
    return {"latent": latent, "target": target, "expand_weight": expand_weight, "expand_bias": expand_bias, "reduce_weight": reduce_weight, "reduce_bias": reduce_bias, "depth_kernel": depth_kernel, "depth_offset": depth_offset, "norm_gain": norm_gain, "norm_shift": norm_shift, "layer_scale": layer_scale}


EPSILON = 1e-06
SQRT_HALF = 0.7071067811865476
INV_ROOT_TAU = 0.3989422804014327

def depthwise(padded, kernel, offset, height, breadth):
    summed = jnp.zeros((height, breadth, padded.shape[2]), jnp.float32) + offset
    for row_off in range(KS):
        for col_off in range(KS):
            summed = summed + kernel[row_off * KS + col_off] * padded[row_off:row_off + height, col_off:col_off + breadth]
    return summed

def depthwise_back(padded_slope, kernel, height, breadth):
    margin = KS // 2
    wide_slope = padded_slope.astype(jnp.float32)
    summed = jnp.zeros((height, breadth, padded_slope.shape[2]), jnp.float32)
    for row_off in range(KS):
        for col_off in range(KS):
            first_row = 2 * margin - row_off
            first_col = 2 * margin - col_off
            summed = summed + kernel[row_off * KS + col_off] * wide_slope[first_row:first_row + height, first_col:first_col + breadth]
    return summed

def kernel_terms(padded, slope, height, breadth):
    pieces = []
    for row_off in range(KS):
        for col_off in range(KS):
            pieces.append(lax.optimization_barrier(jnp.sum(slope * padded[row_off:row_off + height, col_off:col_off + breadth], axis=(0, 1))))
    return jnp.stack(pieces)

def normalize(flat):
    centre = lax.optimization_barrier(jnp.mean(flat, axis=-1, keepdims=True))
    centred = flat - centre
    variance = lax.optimization_barrier(jnp.mean(centred * centred, axis=-1, keepdims=True))
    inverse = lax.rsqrt(variance + EPSILON)
    return (centred * inverse, inverse)

def gelu_slope(hidden):
    return 0.5 * (1.0 + jax.scipy.special.erf(hidden * SQRT_HALF)) + hidden * jnp.exp(-0.5 * hidden * hidden) * INV_ROOT_TAU

def contract_last(left, right):
    return lax.dot_general(left, right, (((1,), (1,)), ((), ())), preferred_element_type=jnp.float32)

def project_forward(mixed, gain, shift, w_expand, b_expand, w_reduce, b_reduce):
    normed, inverse = normalize(mixed)
    inputs = (normed * gain + shift).astype(jnp.bfloat16)
    hidden = jnp.dot(inputs, w_expand, preferred_element_type=jnp.float32) + b_expand
    active = jax.nn.gelu(hidden, approximate=False).astype(jnp.bfloat16)
    branch = jnp.dot(active, w_reduce, preferred_element_type=jnp.float32) + b_reduce
    return (normed, inverse, hidden, branch)

def project_backward(incoming, normed, inverse, hidden, branch, gain, scale, w_expand, w_reduce):
    arrived = incoming.astype(jnp.float32)
    scale_term = lax.optimization_barrier(jnp.sum(arrived * branch, axis=0))
    reduced = (arrived * scale).astype(jnp.bfloat16)
    spread = contract_last(reduced, w_reduce)
    hidden_slope = (spread * gelu_slope(hidden)).astype(jnp.bfloat16)
    normal_slope = contract_last(hidden_slope, w_expand)
    gain_term = lax.optimization_barrier(jnp.sum(normal_slope * normed, axis=0))
    shift_term = lax.optimization_barrier(jnp.sum(normal_slope, axis=0))
    scaled = normal_slope * gain
    slope = (scaled - lax.optimization_barrier(jnp.mean(scaled, axis=-1, keepdims=True)) - normed * lax.optimization_barrier(jnp.mean(scaled * normed, axis=-1, keepdims=True))) * inverse
    offset_term = lax.optimization_barrier(jnp.sum(slope, axis=0))
    return (slope, scale_term, gain_term, shift_term, offset_term)

def reference(latent, target, expand_weight, expand_bias, reduce_weight, reduce_bias, depth_kernel, depth_offset, norm_gain, norm_shift, layer_scale):
    micro_count, height, breadth, channels = latent.shape
    margin = KS // 2
    loss_scale = 1.0 / math.sqrt(micro_count * height * breadth)
    layers = expand_weight.shape[0]
    kernel_acc = [jnp.zeros((KS * KS, channels), jnp.float32) for block_pos in range(layers)]
    offset_acc = [jnp.zeros((channels,), jnp.float32) for block_pos in range(layers)]
    gain_acc = [jnp.zeros((channels,), jnp.float32) for block_pos in range(layers)]
    shift_acc = [jnp.zeros((channels,), jnp.float32) for block_pos in range(layers)]
    scale_acc = [jnp.zeros((channels,), jnp.float32) for block_pos in range(layers)]
    for micro_pos in range(micro_count):
        current = latent[micro_pos]
        records = []
        for block_pos in range(layers):
            framed = jnp.pad(current, ((margin, margin), (0, 0), (0, 0)))
            padded = jnp.pad(framed.astype(jnp.float32), ((0, 0), (margin, margin), (0, 0)))
            mixed = depthwise(padded, depth_kernel[block_pos], depth_offset[block_pos], height, breadth).reshape(-1, channels)
            normed, inverse, hidden, branch = project_forward(mixed, norm_gain[block_pos], norm_shift[block_pos], expand_weight[block_pos], expand_bias[block_pos], reduce_weight[block_pos], reduce_bias[block_pos])
            records.append((padded, normed, inverse, hidden, branch))
            current = (current.astype(jnp.float32) + layer_scale[block_pos] * branch.reshape(height, breadth, channels)).astype(jnp.bfloat16)
        incoming = ((current.astype(jnp.float32) - target[micro_pos].astype(jnp.float32)) * loss_scale).astype(jnp.bfloat16)
        for block_pos in range(layers - 1, -1, -1):
            padded, normed, inverse, hidden, branch = records[block_pos]
            slope, scale_term, gain_term, shift_term, offset_term = project_backward(incoming.reshape(-1, channels), normed, inverse, hidden, branch, norm_gain[block_pos], layer_scale[block_pos], expand_weight[block_pos], reduce_weight[block_pos])
            slope_grid = slope.reshape(height, breadth, channels)
            kernel_acc[block_pos] = kernel_acc[block_pos] + kernel_terms(padded, slope_grid, height, breadth)
            offset_acc[block_pos] = offset_acc[block_pos] + offset_term
            gain_acc[block_pos] = gain_acc[block_pos] + gain_term
            shift_acc[block_pos] = shift_acc[block_pos] + shift_term
            scale_acc[block_pos] = scale_acc[block_pos] + scale_term
            if block_pos > 0:
                slope_low = slope_grid.astype(jnp.bfloat16)
                padded_slope = jnp.pad(slope_low, ((margin, margin), (margin, margin), (0, 0)))
                spread_back = depthwise_back(padded_slope, depth_kernel[block_pos], height, breadth)
                incoming = (incoming.astype(jnp.float32) + spread_back).astype(jnp.bfloat16)
    return (jnp.stack(kernel_acc), jnp.stack(offset_acc), jnp.stack(gain_acc), jnp.stack(shift_acc), jnp.stack(scale_acc))
```

```python
import functools
import math

import jax
import jax.numpy as jnp
from jax import lax
from jax.experimental import pallas as pl
from jax.experimental.pallas import tpu as pltpu
from jax.sharding import PartitionSpec as P

KS = 7
MARGIN = KS // 2
LANES = 128
SIDE = 8
EPSILON = 1e-06
SQRT_HALF = 0.7071067811865476
INV_ROOT_TAU = 0.3989422804014327
MESH = pl.DeviceIdType.MESH


def contract_last(left, right):
    return lax.dot_general(
        left, right, (((1,), (1,)), ((), ())), preferred_element_type=jnp.float32
    )


def eight_rows(value):
    tokens, channels = value.shape
    return value.reshape(tokens // 8, 8, channels).sum(axis=0)


def chain_kernel(
    sections, slabs, loss_scale,
    latent, target, w_expand, b_expand, w_reduce, b_reduce, taps, offset, gain, shift, scale,
    kernel_out, offset_out, gain_out, shift_out, scale_out,
    frame, output, normed_s, inverse_s, bend_s, branch_s,
    cot_in, slope_frame, cot, slope_low, slope_s, grid_s, token_s, pad, taps_next,
    kernel_sum, small_sum, slots,
    fwd_send, edge_send, fwd_recv, bwd_send, bwd_recv, tap_send, tap_recv, sum_send, sum_recv,
):
    sec = lax.axis_index("section")
    row = lax.axis_index("rows")
    micro, height, breadth, channels = latent.shape
    tokens = height * breadth
    hidden_units = w_expand.shape[1]
    piece = 512 if hidden_units % 512 == 0 else LANES
    tall = height + 2 * MARGIN
    first, last = sec == 0, sec == sections - 1
    has_low, has_high = row > 0, row < slabs - 1

    barrier = pltpu.get_barrier_semaphore()
    greeted = jnp.int32(slabs - 1)
    for other in range(slabs):
        @pl.when(row != other)
        def _(other=other):
            pl.semaphore_signal(
                barrier, inc=1, device_id={"section": sec, "rows": other}, device_id_type=MESH
            )
    for ds in (-1, 1):
        for dr in (-1, 0, 1):
            there = (sec + ds >= 0) & (sec + ds < sections) & (row + dr >= 0) & (row + dr < slabs)

            @pl.when(there)
            def _(ds=ds, dr=dr):
                pl.semaphore_signal(
                    barrier, inc=1,
                    device_id={"section": sec + ds, "rows": row + dr}, device_id_type=MESH,
                )
            greeted = greeted + jnp.where(there, 1, 0)
    pl.semaphore_wait(barrier, greeted)

    def remote(source, dest, send, recv, to_sec, to_row):
        return pltpu.make_async_remote_copy(
            src_ref=source, dst_ref=dest, send_sem=send, recv_sem=recv,
            device_id={"section": to_sec, "rows": to_row}, device_id_type=MESH,
        )

    def grid_copies(source, dest, m, send, recv, to_sec):
        low, high = jnp.maximum(row - 1, 0), jnp.minimum(row + 1, slabs - 1)
        return (
            remote(source.at[m], dest.at[m, pl.ds(MARGIN, height)],
                   send.at[m, 0], recv.at[m, 0], to_sec, row),
            remote(source.at[m, pl.ds(height - MARGIN, MARGIN)], dest.at[m, pl.ds(0, MARGIN)],
                   send.at[m, 1], recv.at[m, 1], to_sec, high),
            remote(source.at[m, pl.ds(0, MARGIN)], dest.at[m, pl.ds(MARGIN + height, MARGIN)],
                   send.at[m, 2], recv.at[m, 2], to_sec, low),
        )

    def fwd_copies(m):
        return grid_copies(output, frame, m, fwd_send, fwd_recv, next_sec)

    def edge_copies(m):
        return grid_copies(latent, frame, m, edge_send, fwd_recv, sec)

    next_sec = jnp.minimum(sec + 1, sections - 1)
    prev_sec = jnp.maximum(sec - 1, 0)
    tap_copy = remote(taps, taps_next, tap_send, tap_recv, prev_sec, row)

    @pl.when(sec > 0)
    def _():
        tap_copy.start()

    @pl.when(first)
    def _():
        for m in range(micro):
            _, down, up = edge_copies(m)

            @pl.when(has_high)
            def _():
                down.start()

            @pl.when(has_low)
            def _():
                up.start()
            frame[m, pl.ds(MARGIN, height)] = latent[m]

    edge = jnp.zeros((micro, MARGIN, breadth, channels), jnp.bfloat16)

    @pl.when(row == 0)
    def _():
        frame[:, pl.ds(0, MARGIN)] = edge
        slope_frame[:, pl.ds(0, MARGIN)] = edge

    @pl.when(row == slabs - 1)
    def _():
        frame[:, pl.ds(MARGIN + height, MARGIN)] = edge
        slope_frame[:, pl.ds(MARGIN + height, MARGIN)] = edge

    pad[:, pl.ds(0, SIDE)] = jnp.zeros((tall, SIDE, channels), jnp.float32)
    pad[:, pl.ds(SIDE + breadth, SIDE)] = jnp.zeros((tall, SIDE, channels), jnp.float32)
    kernel_sum[...] = jnp.zeros_like(kernel_sum)
    small_sum[...] = jnp.zeros_like(small_sum)

    def lanes_of(c):
        return pl.ds(pl.multiple_of(c * LANES, LANES), LANES)

    def columns(col_off, lanes):
        return pad[:, pl.ds(SIDE - MARGIN + col_off, breadth), lanes]

    @pl.loop(0, micro)
    def _(m):
        mid, down, up = fwd_copies(m)

        @pl.when(sec > 0)
        def _():
            mid.wait_recv()

        @pl.when(has_low)
        def _():
            down.wait_recv()

        @pl.when(has_high)
        def _():
            up.wait_recv()

        pad[:, pl.ds(SIDE, breadth)] = frame[m].astype(jnp.float32)

        @pl.loop(0, channels // LANES)
        def _(c):
            lanes = lanes_of(c)
            summed = jnp.zeros((height, breadth, LANES), jnp.float32) + offset[:, lanes]
            for b in range(KS):
                column = columns(b, lanes)
                for a in range(KS):
                    summed = summed + taps[pl.ds(KS * a + b, 1), lanes] * column[a : a + height]
            grid_s[:, :, lanes] = summed

        mixed = grid_s[...].reshape(tokens, channels)
        centred = mixed - jnp.mean(mixed, axis=-1, keepdims=True)
        variance = jnp.mean(centred * centred, axis=-1, keepdims=True)
        inverse = lax.rsqrt(variance + EPSILON)
        normed = centred * inverse
        normed_s[m] = normed
        inverse_s[m] = jnp.broadcast_to(inverse, (tokens, LANES))
        inputs = (normed * gain[...] + shift[...]).astype(jnp.bfloat16)
        branch = jnp.zeros((tokens, channels), jnp.float32) + b_reduce[...]
        for f in range(hidden_units // piece):
            units = pl.ds(f * piece, piece)
            hidden = (
                jnp.dot(inputs, w_expand[:, units], preferred_element_type=jnp.float32)
                + b_expand[:, units]
            )
            below = 0.5 * (1.0 + lax.erf(hidden * SQRT_HALF))
            bend_s[m, :, units] = below + hidden * jnp.exp(-0.5 * hidden * hidden) * INV_ROOT_TAU
            active = (hidden * below).astype(jnp.bfloat16)
            branch = branch + jnp.dot(active, w_reduce[units, :], preferred_element_type=jnp.float32)
        branch_s[m] = branch
        source = frame[m, pl.ds(MARGIN, height)].astype(jnp.float32)
        grown = source + (scale[...] * branch).reshape(height, breadth, channels)
        output[m] = grown.astype(jnp.bfloat16)

        @pl.when(sec < sections - 1)
        def _():
            mid.start()

            @pl.when(has_high)
            def _():
                down.start()

            @pl.when(has_low)
            def _():
                up.start()

    @pl.when(sec < sections - 1)
    def _():
        tap_copy.wait_recv()

    def bwd_copies(m):
        return grid_copies(slope_low, slope_frame, m, bwd_send, bwd_recv, prev_sec) + (
            remote(cot.at[m], cot_in.at[m], bwd_send.at[m, 3], bwd_recv.at[m, 3], prev_sec, row),
        )

    @pl.loop(0, micro)
    def _(m):
        mid, down, up, whole = bwd_copies(m)

        @pl.when(last)
        def _():
            gap = output[m].astype(jnp.float32) - target[m].astype(jnp.float32)
            cot[m] = (gap * loss_scale).astype(jnp.bfloat16)

        @pl.when(sec < sections - 1)
        def _():
            mid.wait_recv()
            whole.wait_recv()

            @pl.when(has_low)
            def _():
                down.wait_recv()

            @pl.when(has_high)
            def _():
                up.wait_recv()

            pad[:, pl.ds(SIDE, breadth)] = slope_frame[m].astype(jnp.float32)

            @pl.loop(0, channels // LANES)
            def _(c):
                lanes = lanes_of(c)
                summed = jnp.zeros((height, breadth, LANES), jnp.float32)
                for b in range(KS):
                    column = columns(2 * MARGIN - b, lanes)
                    for a in range(KS):
                        begin = 2 * MARGIN - a
                        summed = (
                            summed
                            + taps_next[pl.ds(KS * a + b, 1), lanes] * column[begin : begin + height]
                        )
                passed = cot_in[m, :, :, lanes].astype(jnp.float32) + summed
                cot[m, :, :, lanes] = passed.astype(jnp.bfloat16)

        arrived = cot[m].astype(jnp.float32).reshape(tokens, channels)
        small_sum[3] += eight_rows(arrived * branch_s[m])
        reduced = (arrived * scale[...]).astype(jnp.bfloat16)
        normal_slope = jnp.zeros((tokens, channels), jnp.float32)
        for f in range(hidden_units // piece):
            units = pl.ds(f * piece, piece)
            spread = contract_last(reduced, w_reduce[units, :])
            hidden_slope = (spread * bend_s[m, :, units]).astype(jnp.bfloat16)
            normal_slope = normal_slope + contract_last(hidden_slope, w_expand[:, units])
        normed = normed_s[m]
        scaled = normal_slope * gain[...]
        token_s[...] = normal_slope
        slope = (
            scaled
            - jnp.mean(scaled, axis=-1, keepdims=True)
            - normed * jnp.mean(scaled * normed, axis=-1, keepdims=True)
        ) * inverse_s[m][:, :1]
        slope_s[...] = slope.reshape(height, breadth, channels)

        @pl.when(sec > 0)
        def _():
            slope_low[m] = slope_s[...].astype(jnp.bfloat16)
            mid.start()
            whole.start()

            @pl.when(has_high)
            def _():
                down.start()

            @pl.when(has_low)
            def _():
                up.start()

        small_sum[0] += eight_rows(slope_s[...].reshape(tokens, channels))
        small_sum[1] += eight_rows(token_s[...] * normed_s[m])
        small_sum[2] += eight_rows(token_s[...])
        pad[:, pl.ds(SIDE, breadth)] = frame[m].astype(jnp.float32)

        @pl.loop(0, channels // LANES)
        def _(c):
            lanes = lanes_of(c)
            own = slope_s[:, :, lanes]
            for b in range(KS):
                column = columns(b, lanes)
                for a in range(KS):
                    term = (own * column[a : a + height]).reshape(tokens, LANES)
                    kernel_sum[KS * a + b, :, lanes] += eight_rows(term)

    spots = KS * KS
    slots[row, pl.ds(0, spots)] = jnp.sum(kernel_sum[...], axis=1)
    slots[row, pl.ds(spots, 4)] = jnp.sum(small_sum[...], axis=1)

    def sum_copy(other, send_at, recv_at):
        return remote(slots.at[row], slots.at[row], sum_send.at[send_at], sum_recv.at[recv_at],
                      sec, other)

    for other in range(slabs):
        @pl.when(row != other)
        def _(other=other):
            sum_copy(other, other, row).start()
    for other in range(slabs):
        @pl.when(row != other)
        def _(other=other):
            copy = remote(slots.at[other], slots.at[other], sum_send.at[other],
                          sum_recv.at[other], sec, other)
            copy.wait_recv()
    total = slots[0]
    for other in range(1, slabs):
        total = total + slots[other]
    kernel_out[...] = total[:spots]
    offset_out[...] = total[spots : spots + 1]
    gain_out[...] = total[spots + 1 : spots + 2]
    shift_out[...] = total[spots + 2 : spots + 3]
    scale_out[...] = total[spots + 3 : spots + 4]

    for other in range(slabs):
        @pl.when(row != other)
        def _(other=other):
            sum_copy(other, other, row).wait_send()

    @pl.when(sec > 0)
    def _():
        tap_copy.wait_send()

    @pl.loop(0, micro)
    def _(m):
        mid, down, up = fwd_copies(m)

        @pl.when(sec < sections - 1)
        def _():
            mid.wait_send()

            @pl.when(has_high)
            def _():
                down.wait_send()

            @pl.when(has_low)
            def _():
                up.wait_send()

        @pl.when(first)
        def _():
            _, edge_down, edge_up = edge_copies(m)

            @pl.when(has_high)
            def _():
                edge_down.wait_send()

            @pl.when(has_low)
            def _():
                edge_up.wait_send()

        mid, down, up, whole = bwd_copies(m)

        @pl.when(sec > 0)
        def _():
            mid.wait_send()
            whole.wait_send()

            @pl.when(has_high)
            def _():
                down.wait_send()

            @pl.when(has_low)
            def _():
                up.wait_send()


def per_device(
    latent, target, expand_weight, expand_bias, reduce_weight, reduce_bias,
    depth_kernel, depth_offset, norm_gain, norm_shift, layer_scale,
):
    sections, slabs = lax.axis_size("section"), lax.axis_size("rows")
    micro, height, breadth, channels = latent.shape
    hidden_units = expand_weight.shape[2]
    tokens = height * breadth
    tall = height + 2 * MARGIN
    spots = KS * KS
    loss_scale = 1.0 / math.sqrt(micro * height * slabs * breadth)
    w_expand = lax.all_gather(expand_weight[0], "rows", axis=0, tiled=True)
    w_reduce = lax.all_gather(reduce_weight[0], "rows", axis=0, tiled=True)
    low, wide = jnp.bfloat16, jnp.float32
    dma, vmem = pltpu.SemaphoreType.DMA, pltpu.VMEM
    found = pl.pallas_call(
        functools.partial(chain_kernel, sections, slabs, loss_scale),
        out_shape=(jax.ShapeDtypeStruct((spots, channels), wide),)
        + (jax.ShapeDtypeStruct((1, channels), wide),) * 4,
        in_specs=[pl.BlockSpec(memory_space=vmem)] * 11,
        out_specs=(pl.BlockSpec(memory_space=vmem),) * 5,
        scratch_shapes=[
            vmem((micro, tall, breadth, channels), low),
            vmem((micro, height, breadth, channels), low),
            vmem((micro, tokens, channels), wide),
            vmem((micro, tokens, LANES), wide),
            vmem((micro, tokens, hidden_units), wide),
            vmem((micro, tokens, channels), wide),
            vmem((micro, height, breadth, channels), low),
            vmem((micro, tall, breadth, channels), low),
            vmem((micro, height, breadth, channels), low),
            vmem((micro, height, breadth, channels), low),
            vmem((height, breadth, channels), wide),
            vmem((height, breadth, channels), wide),
            vmem((tokens, channels), wide),
            vmem((tall, breadth + 2 * SIDE, channels), wide),
            vmem((spots, channels), wide),
            vmem((spots, 8, channels), wide),
            vmem((4, 8, channels), wide),
            vmem((slabs, spots + 4, channels), wide),
            dma((micro, 3)), dma((micro, 3)), dma((micro, 3)),
            dma((micro, 4)), dma((micro, 4)),
            dma, dma,
            dma((slabs,)), dma((slabs,)),
        ],
        compiler_params=pltpu.CompilerParams(
            collective_id=0, has_side_effects=True, vmem_limit_bytes=48 * 1024 * 1024
        ),
        name="block_chain",
    )(
        latent, target, w_expand, expand_bias, w_reduce, reduce_bias,
        depth_kernel[0], depth_offset, norm_gain, norm_shift, layer_scale,
    )
    return (found[0][None],) + tuple(found[1:])


def solution(mesh):
    image = P("groups", "rows", None, None)
    matrix, vector = P("section", "rows", None), P("section", None)
    both = ("groups", "section")
    return jax.shard_map(
        per_device,
        mesh=mesh,
        in_specs=(
            image, image, matrix, vector, matrix, vector,
            P("section", None, None), vector, vector, vector, vector,
        ),
        out_specs=(P(both, None, None),) + (P(both, None),) * 4,
        check_vma=False,
    )
```

```python
import functools
import math

import jax
import jax.numpy as jnp
from jax import lax
from jax.experimental import pallas as pl
from jax.experimental.pallas import tpu as pltpu
from jax.sharding import PartitionSpec as P

KS = 7
MARGIN = KS // 2
LANES = 128
SIDE = 8
EPSILON = 1e-06
SQRT_HALF = 0.7071067811865476
INV_ROOT_TAU = 0.3989422804014327
MESH = pl.DeviceIdType.MESH


def contract_last(left, right):
    return lax.dot_general(
        left, right, (((1,), (1,)), ((), ())), preferred_element_type=jnp.float32
    )


def eight_rows(value):
    tokens, channels = value.shape
    return value.reshape(tokens // 8, 8, channels).sum(axis=0)


def chain_kernel(
    sections, slabs, copies, gathered, loss_scale,
    latent_in, target_in, w_expand_in, b_expand_in, w_reduce_in, b_reduce_in,
    taps_in, offset_in, gain_in, shift_in, scale_in,
    kernel_out, offset_out, gain_out, shift_out, scale_out,
    latent, target, w_expand, b_expand, w_reduce, b_reduce, taps, offset, gain, shift, scale,
    frame, output, normed_s, inverse_s, bend_s, branch_s,
    cot_in, slope_frame, cot, slope_low, slope_s, grid_s, token_s, pad, taps_next,
    kernel_sum, small_sum, slots,
    fwd_send, edge_send, fwd_recv, bwd_send, bwd_recv, tap_send, tap_recv, sum_send, sum_recv, load_sem, part_send, part_recv,
):
    sec = lax.axis_index("section")
    row = lax.axis_index("rows")
    micro, height, breadth, channels = latent.shape
    tokens = height * breadth
    hidden_units = w_expand.shape[1]
    piece = 512 if hidden_units % 512 == 0 else LANES
    tall = height + 2 * MARGIN
    first, last = sec == 0, sec == sections - 1
    has_low, has_high = row > 0, row < slabs - 1

    group = lax.axis_index("groups")

    def rows_of(whole, shard):
        depth = whole.shape[0] // slabs
        return pl.ds(pl.multiple_of(shard * depth, 16), depth)

    local = []
    for source, dest in (
        (w_expand_in, w_expand), (w_reduce_in, w_reduce), (taps_in, taps), (latent_in, latent),
        (target_in, target), (b_expand_in, b_expand), (b_reduce_in, b_reduce),
        (offset_in, offset), (gain_in, gain), (shift_in, shift), (scale_in, scale),
    ):
        if len(local) < 2 and not gathered:
            dest = dest.at[rows_of(dest, row)]
        local.append(pltpu.make_async_copy(source, dest, load_sem.at[len(local)]))
        local[-1].start()

    barrier = pltpu.get_barrier_semaphore()
    greeted = jnp.int32(slabs - 1)
    for other in range(slabs):
        @pl.when(row != other)
        def _(other=other):
            pl.semaphore_signal(
                barrier, inc=1, device_id={"section": sec, "rows": other}, device_id_type=MESH
            )
    for ds in (-1, 1):
        for dr in (-1, 0, 1):
            there = (sec + ds >= 0) & (sec + ds < sections) & (row + dr >= 0) & (row + dr < slabs)

            @pl.when(there)
            def _(ds=ds, dr=dr):
                pl.semaphore_signal(
                    barrier, inc=1,
                    device_id={"section": sec + ds, "rows": row + dr}, device_id_type=MESH,
                )
            greeted = greeted + jnp.where(there, 1, 0)
    if not gathered:
        for other in range(copies):
            @pl.when(group != other)
            def _(other=other):
                pl.semaphore_signal(
                    barrier, inc=1, device_id={"groups": other}, device_id_type=MESH
                )
        greeted = greeted + (copies - 1)
    pl.semaphore_wait(barrier, greeted)

    weights = ((w_expand_in, w_expand), (w_reduce_in, w_reduce))

    def part_of(t, shard, part):
        width = weights[t][1].shape[1] // copies
        return rows_of(weights[t][1], shard), pl.ds(pl.multiple_of(part * width, LANES), width)

    def along(t, shard, onward, own=False):
        rows, cols = part_of(t, shard, group)
        dest = weights[t][1].at[rows, cols]
        source = weights[t][0].at[:, cols] if own else dest
        to_row = jnp.minimum(row + 1, slabs - 1) if onward == 0 else jnp.maximum(row - 1, 0)
        return pltpu.make_async_remote_copy(
            src_ref=source, dst_ref=dest,
            send_sem=part_send.at[t, shard, onward], recv_sem=part_recv.at[t, shard, group],
            device_id={"rows": to_row}, device_id_type=MESH,
        )

    def across(t, shard, other, arriving=False):
        part = other if arriving else group
        block = weights[t][1].at[part_of(t, shard, part)]
        return pltpu.make_async_remote_copy(
            src_ref=block, dst_ref=block,
            send_sem=part_send.at[t, shard, 2 + other], recv_sem=part_recv.at[t, shard, part],
            device_id={"groups": other}, device_id_type=MESH,
        )

    def each_other_copy(act):
        for other in range(copies):
            @pl.when(group != other)
            def _(other=other):
                act(other)

    def start_parts():
        for t in range(2):
            @pl.when(row < slabs - 1)
            def _(t=t):
                along(t, row, 0, own=True).start()

            @pl.when(row > 0)
            def _(t=t):
                along(t, row, 1, own=True).start()

    def pass_parts():
        for t in range(2):
            for far in range(1, slabs):
                @pl.when(row - far >= 0)
                def _(t=t, far=far):
                    shard = row - far
                    along(t, shard, 0).wait_recv()

                    @pl.when(row < slabs - 1)
                    def _():
                        along(t, shard, 0).start()
                    each_other_copy(lambda other: across(t, shard, other).start())

                @pl.when(row + far < slabs)
                def _(t=t, far=far):
                    shard = row + far
                    along(t, shard, 1).wait_recv()

                    @pl.when(row > 0)
                    def _():
                        along(t, shard, 1).start()
                    each_other_copy(lambda other: across(t, shard, other).start())
        for t in range(2):
            for shard in range(slabs):
                @pl.when(row != shard)
                def _(t=t, shard=shard):
                    each_other_copy(lambda other: across(t, shard, other, True).wait_recv())

    def finish_parts():
        for t in range(2):
            for shard in range(slabs):
                @pl.when((row >= shard) & (row < slabs - 1))
                def _(t=t, shard=shard):
                    along(t, shard, 0).wait_send()

                @pl.when((row <= shard) & (row > 0))
                def _(t=t, shard=shard):
                    along(t, shard, 1).wait_send()

                @pl.when(row != shard)
                def _(t=t, shard=shard):
                    each_other_copy(lambda other: across(t, shard, other).wait_send())

    if not gathered:
        start_parts()
    for copy in local:
        copy.wait()

    def remote(source, dest, send, recv, to_sec, to_row):
        return pltpu.make_async_remote_copy(
            src_ref=source, dst_ref=dest, send_sem=send, recv_sem=recv,
            device_id={"section": to_sec, "rows": to_row}, device_id_type=MESH,
        )

    def grid_copies(source, dest, m, send, recv, to_sec):
        low, high = jnp.maximum(row - 1, 0), jnp.minimum(row + 1, slabs - 1)
        return (
            remote(source.at[m], dest.at[m, pl.ds(MARGIN, height)],
                   send.at[m, 0], recv.at[m, 0], to_sec, row),
            remote(source.at[m, pl.ds(height - MARGIN, MARGIN)], dest.at[m, pl.ds(0, MARGIN)],
                   send.at[m, 1], recv.at[m, 1], to_sec, high),
            remote(source.at[m, pl.ds(0, MARGIN)], dest.at[m, pl.ds(MARGIN + height, MARGIN)],
                   send.at[m, 2], recv.at[m, 2], to_sec, low),
        )

    def fwd_copies(m):
        return grid_copies(output, frame, m, fwd_send, fwd_recv, next_sec)

    def edge_copies(m):
        return grid_copies(latent, frame, m, edge_send, fwd_recv, sec)

    next_sec = jnp.minimum(sec + 1, sections - 1)
    prev_sec = jnp.maximum(sec - 1, 0)
    tap_copy = remote(taps, taps_next, tap_send, tap_recv, prev_sec, row)

    @pl.when(sec > 0)
    def _():
        tap_copy.start()

    @pl.when(first)
    def _():
        for m in range(micro):
            _, down, up = edge_copies(m)

            @pl.when(has_high)
            def _():
                down.start()

            @pl.when(has_low)
            def _():
                up.start()
            frame[m, pl.ds(MARGIN, height)] = latent[m]

    edge = jnp.zeros((micro, MARGIN, breadth, channels), jnp.bfloat16)

    @pl.when(row == 0)
    def _():
        frame[:, pl.ds(0, MARGIN)] = edge
        slope_frame[:, pl.ds(0, MARGIN)] = edge

    @pl.when(row == slabs - 1)
    def _():
        frame[:, pl.ds(MARGIN + height, MARGIN)] = edge
        slope_frame[:, pl.ds(MARGIN + height, MARGIN)] = edge

    pad[:, pl.ds(0, SIDE)] = jnp.zeros((tall, SIDE, channels), jnp.float32)
    pad[:, pl.ds(SIDE + breadth, SIDE)] = jnp.zeros((tall, SIDE, channels), jnp.float32)
    kernel_sum[...] = jnp.zeros_like(kernel_sum)
    small_sum[...] = jnp.zeros_like(small_sum)
    if not gathered:
        pass_parts()

    def lanes_of(c):
        return pl.ds(pl.multiple_of(c * LANES, LANES), LANES)

    def columns(col_off, lanes):
        return pad[:, pl.ds(SIDE - MARGIN + col_off, breadth), lanes]

    @pl.loop(0, micro)
    def _(m):
        mid, down, up = fwd_copies(m)

        @pl.when(sec > 0)
        def _():
            mid.wait_recv()

        @pl.when(has_low)
        def _():
            down.wait_recv()

        @pl.when(has_high)
        def _():
            up.wait_recv()

        pad[:, pl.ds(SIDE, breadth)] = frame[m].astype(jnp.float32)

        @pl.loop(0, channels // LANES)
        def _(c):
            lanes = lanes_of(c)
            summed = jnp.zeros((height, breadth, LANES), jnp.float32) + offset[:, lanes]
            for b in range(KS):
                column = columns(b, lanes)
                for a in range(KS):
                    summed = summed + taps[pl.ds(KS * a + b, 1), lanes] * column[a : a + height]
            grid_s[:, :, lanes] = summed

        mixed = grid_s[...].reshape(tokens, channels)
        centred = mixed - jnp.mean(mixed, axis=-1, keepdims=True)
        variance = jnp.mean(centred * centred, axis=-1, keepdims=True)
        inverse = lax.rsqrt(variance + EPSILON)
        normed = centred * inverse
        normed_s[m] = normed
        inverse_s[m] = jnp.broadcast_to(inverse, (tokens, LANES))
        inputs = (normed * gain[...] + shift[...]).astype(jnp.bfloat16)
        branch = jnp.zeros((tokens, channels), jnp.float32) + b_reduce[...]
        for f in range(hidden_units // piece):
            units = pl.ds(f * piece, piece)
            hidden = (
                jnp.dot(inputs, w_expand[:, units], preferred_element_type=jnp.float32)
                + b_expand[:, units]
            )
            below = 0.5 * (1.0 + lax.erf(hidden * SQRT_HALF))
            bend_s[m, :, units] = below + hidden * jnp.exp(-0.5 * hidden * hidden) * INV_ROOT_TAU
            active = (hidden * below).astype(jnp.bfloat16)
            branch = branch + jnp.dot(active, w_reduce[units, :], preferred_element_type=jnp.float32)
        branch_s[m] = branch
        source = frame[m, pl.ds(MARGIN, height)].astype(jnp.float32)
        grown = source + (scale[...] * branch).reshape(height, breadth, channels)
        output[m] = grown.astype(jnp.bfloat16)

        @pl.when(sec < sections - 1)
        def _():
            mid.start()

            @pl.when(has_high)
            def _():
                down.start()

            @pl.when(has_low)
            def _():
                up.start()

    @pl.when(sec < sections - 1)
    def _():
        tap_copy.wait_recv()

    def bwd_copies(m):
        return grid_copies(slope_low, slope_frame, m, bwd_send, bwd_recv, prev_sec) + (
            remote(cot.at[m], cot_in.at[m], bwd_send.at[m, 3], bwd_recv.at[m, 3], prev_sec, row),
        )

    @pl.loop(0, micro)
    def _(m):
        mid, down, up, whole = bwd_copies(m)

        @pl.when(last)
        def _():
            gap = output[m].astype(jnp.float32) - target[m].astype(jnp.float32)
            cot[m] = (gap * loss_scale).astype(jnp.bfloat16)

        @pl.when(sec < sections - 1)
        def _():
            mid.wait_recv()
            whole.wait_recv()

            @pl.when(has_low)
            def _():
                down.wait_recv()

            @pl.when(has_high)
            def _():
                up.wait_recv()

            pad[:, pl.ds(SIDE, breadth)] = slope_frame[m].astype(jnp.float32)

            @pl.loop(0, channels // LANES)
            def _(c):
                lanes = lanes_of(c)
                summed = jnp.zeros((height, breadth, LANES), jnp.float32)
                for b in range(KS):
                    column = columns(2 * MARGIN - b, lanes)
                    for a in range(KS):
                        begin = 2 * MARGIN - a
                        summed = (
                            summed
                            + taps_next[pl.ds(KS * a + b, 1), lanes] * column[begin : begin + height]
                        )
                passed = cot_in[m, :, :, lanes].astype(jnp.float32) + summed
                cot[m, :, :, lanes] = passed.astype(jnp.bfloat16)

        arrived = cot[m].astype(jnp.float32).reshape(tokens, channels)
        small_sum[3] += eight_rows(arrived * branch_s[m])
        reduced = (arrived * scale[...]).astype(jnp.bfloat16)
        normal_slope = jnp.zeros((tokens, channels), jnp.float32)
        for f in range(hidden_units // piece):
            units = pl.ds(f * piece, piece)
            spread = contract_last(reduced, w_reduce[units, :])
            hidden_slope = (spread * bend_s[m, :, units]).astype(jnp.bfloat16)
            normal_slope = normal_slope + contract_last(hidden_slope, w_expand[:, units])
        normed = normed_s[m]
        scaled = normal_slope * gain[...]
        token_s[...] = normal_slope
        slope = (
            scaled
            - jnp.mean(scaled, axis=-1, keepdims=True)
            - normed * jnp.mean(scaled * normed, axis=-1, keepdims=True)
        ) * inverse_s[m][:, :1]
        slope_s[...] = slope.reshape(height, breadth, channels)

        @pl.when(sec > 0)
        def _():
            slope_low[m] = slope_s[...].astype(jnp.bfloat16)
            mid.start()
            whole.start()

            @pl.when(has_high)
            def _():
                down.start()

            @pl.when(has_low)
            def _():
                up.start()

        small_sum[0] += eight_rows(slope_s[...].reshape(tokens, channels))
        small_sum[1] += eight_rows(token_s[...] * normed_s[m])
        small_sum[2] += eight_rows(token_s[...])
        pad[:, pl.ds(SIDE, breadth)] = frame[m].astype(jnp.float32)

        @pl.loop(0, channels // LANES)
        def _(c):
            lanes = lanes_of(c)
            own = slope_s[:, :, lanes]
            for b in range(KS):
                column = columns(b, lanes)
                for a in range(KS):
                    term = (own * column[a : a + height]).reshape(tokens, LANES)
                    kernel_sum[KS * a + b, :, lanes] += eight_rows(term)

    spots = KS * KS
    slots[row, pl.ds(0, spots)] = jnp.sum(kernel_sum[...], axis=1)
    slots[row, pl.ds(spots, 4)] = jnp.sum(small_sum[...], axis=1)

    def sum_copy(other, send_at, recv_at):
        return remote(slots.at[row], slots.at[row], sum_send.at[send_at], sum_recv.at[recv_at],
                      sec, other)

    for other in range(slabs):
        @pl.when(row != other)
        def _(other=other):
            sum_copy(other, other, row).start()
    for other in range(slabs):
        @pl.when(row != other)
        def _(other=other):
            copy = remote(slots.at[other], slots.at[other], sum_send.at[other],
                          sum_recv.at[other], sec, other)
            copy.wait_recv()
    total = slots[0]
    for other in range(1, slabs):
        total = total + slots[other]
    kernel_out[...] = total[:spots]
    offset_out[...] = total[spots : spots + 1]
    gain_out[...] = total[spots + 1 : spots + 2]
    shift_out[...] = total[spots + 2 : spots + 3]
    scale_out[...] = total[spots + 3 : spots + 4]

    if not gathered:
        finish_parts()
    for other in range(slabs):
        @pl.when(row != other)
        def _(other=other):
            sum_copy(other, other, row).wait_send()

    @pl.when(sec > 0)
    def _():
        tap_copy.wait_send()

    @pl.loop(0, micro)
    def _(m):
        mid, down, up = fwd_copies(m)

        @pl.when(sec < sections - 1)
        def _():
            mid.wait_send()

            @pl.when(has_high)
            def _():
                down.wait_send()

            @pl.when(has_low)
            def _():
                up.wait_send()

        @pl.when(first)
        def _():
            _, edge_down, edge_up = edge_copies(m)

            @pl.when(has_high)
            def _():
                edge_down.wait_send()

            @pl.when(has_low)
            def _():
                edge_up.wait_send()

        mid, down, up, whole = bwd_copies(m)

        @pl.when(sec > 0)
        def _():
            mid.wait_send()
            whole.wait_send()

            @pl.when(has_high)
            def _():
                down.wait_send()

            @pl.when(has_low)
            def _():
                up.wait_send()


def per_device(
    latent, target, expand_weight, expand_bias, reduce_weight, reduce_bias,
    depth_kernel, depth_offset, norm_gain, norm_shift, layer_scale,
):
    sections, slabs = lax.axis_size("section"), lax.axis_size("rows")
    micro, height, breadth, channels = latent.shape
    hidden_units = expand_weight.shape[2]
    tokens = height * breadth
    tall = height + 2 * MARGIN
    spots = KS * KS
    loss_scale = 1.0 / math.sqrt(micro * height * slabs * breadth)
    copies = lax.axis_size("groups")
    w_expand, w_reduce = expand_weight[0], reduce_weight[0]
    aligned = all(
        held.shape[0] % 16 == 0 and held.shape[1] % (LANES * copies) == 0
        for held in (w_expand, w_reduce)
    )
    if not aligned:
        w_expand = lax.all_gather(w_expand, "rows", axis=0, tiled=True)
        w_reduce = lax.all_gather(w_reduce, "rows", axis=0, tiled=True)
    low, wide = jnp.bfloat16, jnp.float32
    dma, vmem = pltpu.SemaphoreType.DMA, pltpu.VMEM
    found = pl.pallas_call(
        functools.partial(chain_kernel, sections, slabs, copies, not aligned, loss_scale),
        out_shape=(jax.ShapeDtypeStruct((spots, channels), wide),)
        + (jax.ShapeDtypeStruct((1, channels), wide),) * 4,
        in_specs=[pl.BlockSpec(memory_space=pltpu.HBM)] * 11,
        out_specs=(pl.BlockSpec(memory_space=vmem),) * 5,
        scratch_shapes=[
            vmem(latent.shape, low), vmem(target.shape, low),
            vmem((channels, hidden_units), low), vmem((1, hidden_units), wide),
            vmem((hidden_units, channels), low), vmem((1, channels), wide),
            vmem((spots, channels), wide),
            vmem((1, channels), wide), vmem((1, channels), wide),
            vmem((1, channels), wide), vmem((1, channels), wide),
            vmem((micro, tall, breadth, channels), low),
            vmem((micro, height, breadth, channels), low),
            vmem((micro, tokens, channels), wide),
            vmem((micro, tokens, LANES), wide),
            vmem((micro, tokens, hidden_units), wide),
            vmem((micro, tokens, channels), wide),
            vmem((micro, height, breadth, channels), low),
            vmem((micro, tall, breadth, channels), low),
            vmem((micro, height, breadth, channels), low),
            vmem((micro, height, breadth, channels), low),
            vmem((height, breadth, channels), wide),
            vmem((height, breadth, channels), wide),
            vmem((tokens, channels), wide),
            vmem((tall, breadth + 2 * SIDE, channels), wide),
            vmem((spots, channels), wide),
            vmem((spots, 8, channels), wide),
            vmem((4, 8, channels), wide),
            vmem((slabs, spots + 4, channels), wide),
            dma((micro, 3)), dma((micro, 3)), dma((micro, 3)),
            dma((micro, 4)), dma((micro, 4)),
            dma, dma,
            dma((slabs,)), dma((slabs,)),
            dma((11,)), dma((2, slabs, 2 + copies)), dma((2, slabs, copies)),
        ],
        compiler_params=pltpu.CompilerParams(
            collective_id=0, has_side_effects=True, vmem_limit_bytes=48 * 1024 * 1024
        ),
        name="block_chain",
    )(
        latent, target, w_expand, expand_bias, w_reduce, reduce_bias,
        depth_kernel[0], depth_offset, norm_gain, norm_shift, layer_scale,
    )
    return (found[0][None],) + tuple(found[1:])


def solution(mesh):
    image = P("groups", "rows", None, None)
    matrix, vector = P("section", "rows", None), P("section", None)
    both = ("groups", "section")
    return jax.shard_map(
        per_device,
        mesh=mesh,
        in_specs=(
            image, image, matrix, vector, matrix, vector,
            P("section", None, None), vector, vector, vector, vector,
        ),
        out_specs=(P(both, None, None),) + (P(both, None),) * 4,
        check_vma=False,
    )
```

```python
import functools
import math

import jax
import jax.numpy as jnp
from jax import lax
from jax.experimental import pallas as pl
from jax.experimental.pallas import tpu as pltpu
from jax.sharding import PartitionSpec as P

KS = 7
MARGIN = KS // 2
LANES = 128
SIDE = 8
EPSILON = 1e-06
SQRT_HALF = 0.7071067811865476
INV_ROOT_TAU = 0.3989422804014327
MESH = pl.DeviceIdType.MESH


def contract_last(left, right):
    return lax.dot_general(
        left, right, (((1,), (1,)), ((), ())), preferred_element_type=jnp.float32
    )


def eight_rows(value):
    tokens, channels = value.shape
    return value.reshape(tokens // 8, 8, channels).sum(axis=0)


def chain_kernel(
    sections, slabs, copies, gathered, loss_scale,
    latent_in, target_in, w_expand_in, b_expand_in, w_reduce_in, b_reduce_in,
    taps_in, offset_in, gain_in, shift_in, scale_in,
    kernel_out, offset_out, gain_out, shift_out, scale_out,
    latent, target, w_expand, b_expand, w_reduce, b_reduce, taps, offset, gain, shift, scale,
    frame, output, normed_s, inverse_s, bend_s, branch_s,
    cot_in, slope_frame, cot, slope_low, slope_s, grid_s, token_s, pad, taps_next,
    kernel_sum, small_sum, parts, slots, sums,
    fwd_send, edge_send, fwd_recv, bwd_send, bwd_recv, tap_send, tap_recv, sum_send, sum_recv, whole_send, whole_recv,
    load_sem, part_send, part_recv,
):
    sec = lax.axis_index("section")
    row = lax.axis_index("rows")
    micro, height, breadth, channels = latent.shape
    tokens = height * breadth
    hidden_units = w_expand.shape[1]
    piece = 512 if hidden_units % 512 == 0 else LANES
    tall = height + 2 * MARGIN
    first, last = sec == 0, sec == sections - 1
    has_low, has_high = row > 0, row < slabs - 1

    group = lax.axis_index("groups")

    def rows_of(whole, shard):
        depth = whole.shape[0] // slabs
        return pl.ds(pl.multiple_of(shard * depth, 16), depth)

    local = []
    for source, dest in (
        (w_expand_in, w_expand), (w_reduce_in, w_reduce), (taps_in, taps), (latent_in, latent),
        (target_in, target), (b_expand_in, b_expand), (b_reduce_in, b_reduce),
        (offset_in, offset), (gain_in, gain), (shift_in, shift), (scale_in, scale),
    ):
        if len(local) < 2 and not gathered:
            dest = dest.at[rows_of(dest, row)]
        local.append(pltpu.make_async_copy(source, dest, load_sem.at[len(local)]))
        local[-1].start()

    barrier = pltpu.get_barrier_semaphore()
    greeted = jnp.int32(slabs - 1)
    for other in range(slabs):
        @pl.when(row != other)
        def _(other=other):
            pl.semaphore_signal(
                barrier, inc=1, device_id={"section": sec, "rows": other}, device_id_type=MESH
            )
    for ds in (-1, 1):
        for dr in (-1, 0, 1):
            there = (sec + ds >= 0) & (sec + ds < sections) & (row + dr >= 0) & (row + dr < slabs)

            @pl.when(there)
            def _(ds=ds, dr=dr):
                pl.semaphore_signal(
                    barrier, inc=1,
                    device_id={"section": sec + ds, "rows": row + dr}, device_id_type=MESH,
                )
            greeted = greeted + jnp.where(there, 1, 0)
    if not gathered:
        for other in range(copies):
            @pl.when(group != other)
            def _(other=other):
                pl.semaphore_signal(
                    barrier, inc=1, device_id={"groups": other}, device_id_type=MESH
                )
        greeted = greeted + (copies - 1)
    pl.semaphore_wait(barrier, greeted)

    weights = ((w_expand_in, w_expand), (w_reduce_in, w_reduce))

    def part_of(t, shard, part):
        width = weights[t][1].shape[1] // copies
        return rows_of(weights[t][1], shard), pl.ds(pl.multiple_of(part * width, LANES), width)

    def along(t, shard, onward, own=False):
        rows, cols = part_of(t, shard, group)
        dest = weights[t][1].at[rows, cols]
        source = weights[t][0].at[:, cols] if own else dest
        to_row = jnp.minimum(row + 1, slabs - 1) if onward == 0 else jnp.maximum(row - 1, 0)
        return pltpu.make_async_remote_copy(
            src_ref=source, dst_ref=dest,
            send_sem=part_send.at[t, shard, onward], recv_sem=part_recv.at[t, shard, group],
            device_id={"rows": to_row}, device_id_type=MESH,
        )

    def across(t, shard, other, arriving=False):
        part = other if arriving else group
        block = weights[t][1].at[part_of(t, shard, part)]
        return pltpu.make_async_remote_copy(
            src_ref=block, dst_ref=block,
            send_sem=part_send.at[t, shard, 2 + other], recv_sem=part_recv.at[t, shard, part],
            device_id={"groups": other}, device_id_type=MESH,
        )

    def each_other_copy(act):
        for other in range(copies):
            @pl.when(group != other)
            def _(other=other):
                act(other)

    def start_parts():
        for t in range(2):
            @pl.when(row < slabs - 1)
            def _(t=t):
                along(t, row, 0, own=True).start()

            @pl.when(row > 0)
            def _(t=t):
                along(t, row, 1, own=True).start()

    def pass_parts():
        for t in range(2):
            for far in range(1, slabs):
                @pl.when(row - far >= 0)
                def _(t=t, far=far):
                    shard = row - far
                    along(t, shard, 0).wait_recv()

                    @pl.when(row < slabs - 1)
                    def _():
                        along(t, shard, 0).start()
                    each_other_copy(lambda other: across(t, shard, other).start())

                @pl.when(row + far < slabs)
                def _(t=t, far=far):
                    shard = row + far
                    along(t, shard, 1).wait_recv()

                    @pl.when(row > 0)
                    def _():
                        along(t, shard, 1).start()
                    each_other_copy(lambda other: across(t, shard, other).start())
        for t in range(2):
            for shard in range(slabs):
                @pl.when(row != shard)
                def _(t=t, shard=shard):
                    each_other_copy(lambda other: across(t, shard, other, True).wait_recv())

    def finish_parts():
        for t in range(2):
            for shard in range(slabs):
                @pl.when((row >= shard) & (row < slabs - 1))
                def _(t=t, shard=shard):
                    along(t, shard, 0).wait_send()

                @pl.when((row <= shard) & (row > 0))
                def _(t=t, shard=shard):
                    along(t, shard, 1).wait_send()

                @pl.when(row != shard)
                def _(t=t, shard=shard):
                    each_other_copy(lambda other: across(t, shard, other).wait_send())

    if not gathered:
        start_parts()
    for copy in local:
        copy.wait()

    def remote(source, dest, send, recv, to_sec, to_row):
        return pltpu.make_async_remote_copy(
            src_ref=source, dst_ref=dest, send_sem=send, recv_sem=recv,
            device_id={"section": to_sec, "rows": to_row}, device_id_type=MESH,
        )

    def grid_copies(source, dest, m, send, recv, to_sec):
        low, high = jnp.maximum(row - 1, 0), jnp.minimum(row + 1, slabs - 1)
        return (
            remote(source.at[m], dest.at[m, pl.ds(MARGIN, height)],
                   send.at[m, 0], recv.at[m, 0], to_sec, row),
            remote(source.at[m, pl.ds(height - MARGIN, MARGIN)], dest.at[m, pl.ds(0, MARGIN)],
                   send.at[m, 1], recv.at[m, 1], to_sec, high),
            remote(source.at[m, pl.ds(0, MARGIN)], dest.at[m, pl.ds(MARGIN + height, MARGIN)],
                   send.at[m, 2], recv.at[m, 2], to_sec, low),
        )

    def fwd_copies(m):
        return grid_copies(output, frame, m, fwd_send, fwd_recv, next_sec)

    def edge_copies(m):
        return grid_copies(latent, frame, m, edge_send, fwd_recv, sec)

    next_sec = jnp.minimum(sec + 1, sections - 1)
    prev_sec = jnp.maximum(sec - 1, 0)
    tap_copy = remote(taps, taps_next, tap_send, tap_recv, prev_sec, row)

    @pl.when(sec > 0)
    def _():
        tap_copy.start()

    @pl.when(first)
    def _():
        for m in range(micro):
            _, down, up = edge_copies(m)

            @pl.when(has_high)
            def _():
                down.start()

            @pl.when(has_low)
            def _():
                up.start()
            frame[m, pl.ds(MARGIN, height)] = latent[m]

    edge = jnp.zeros((micro, MARGIN, breadth, channels), jnp.bfloat16)

    @pl.when(row == 0)
    def _():
        frame[:, pl.ds(0, MARGIN)] = edge
        slope_frame[:, pl.ds(0, MARGIN)] = edge

    @pl.when(row == slabs - 1)
    def _():
        frame[:, pl.ds(MARGIN + height, MARGIN)] = edge
        slope_frame[:, pl.ds(MARGIN + height, MARGIN)] = edge

    pad[:, pl.ds(0, SIDE)] = jnp.zeros((tall, SIDE, channels), jnp.float32)
    pad[:, pl.ds(SIDE + breadth, SIDE)] = jnp.zeros((tall, SIDE, channels), jnp.float32)
    kernel_sum[...] = jnp.zeros_like(kernel_sum)
    small_sum[...] = jnp.zeros_like(small_sum)
    if not gathered:
        pass_parts()

    def lanes_of(c):
        return pl.ds(pl.multiple_of(c * LANES, LANES), LANES)

    def columns(col_off, lanes):
        return pad[:, pl.ds(SIDE - MARGIN + col_off, breadth), lanes]

    @pl.loop(0, micro)
    def _(m):
        mid, down, up = fwd_copies(m)

        @pl.when(sec > 0)
        def _():
            mid.wait_recv()

        @pl.when(has_low)
        def _():
            down.wait_recv()

        @pl.when(has_high)
        def _():
            up.wait_recv()

        pad[:, pl.ds(SIDE, breadth)] = frame[m].astype(jnp.float32)

        @pl.loop(0, channels // LANES)
        def _(c):
            lanes = lanes_of(c)
            summed = jnp.zeros((height, breadth, LANES), jnp.float32) + offset[:, lanes]
            for b in range(KS):
                column = columns(b, lanes)
                for a in range(KS):
                    summed = summed + taps[KS * a + b, :, lanes] * column[a : a + height]
            grid_s[:, :, lanes] = summed

        mixed = grid_s[...].reshape(tokens, channels)
        centred = mixed - jnp.mean(mixed, axis=-1, keepdims=True)
        variance = jnp.mean(centred * centred, axis=-1, keepdims=True)
        inverse = lax.rsqrt(variance + EPSILON)
        normed = centred * inverse
        normed_s[m] = normed
        inverse_s[m] = jnp.broadcast_to(inverse, (tokens, LANES))
        inputs = (normed * gain[...] + shift[...]).astype(jnp.bfloat16)
        branch = jnp.zeros((tokens, channels), jnp.float32) + b_reduce[...]
        for f in range(hidden_units // piece):
            units = pl.ds(f * piece, piece)
            hidden = (
                jnp.dot(inputs, w_expand[:, units], preferred_element_type=jnp.float32)
                + b_expand[:, units]
            )
            below = 0.5 * (1.0 + lax.erf(hidden * SQRT_HALF))
            bend_s[m, :, units] = below + hidden * jnp.exp(-0.5 * hidden * hidden) * INV_ROOT_TAU
            active = (hidden * below).astype(jnp.bfloat16)
            branch = branch + jnp.dot(active, w_reduce[units, :], preferred_element_type=jnp.float32)
        branch_s[m] = branch
        source = frame[m, pl.ds(MARGIN, height)].astype(jnp.float32)
        grown = source + (scale[...] * branch).reshape(height, breadth, channels)
        output[m] = grown.astype(jnp.bfloat16)

        @pl.when(sec < sections - 1)
        def _():
            mid.start()

            @pl.when(has_high)
            def _():
                down.start()

            @pl.when(has_low)
            def _():
                up.start()

    @pl.when(sec < sections - 1)
    def _():
        tap_copy.wait_recv()

    def bwd_copies(m):
        return grid_copies(slope_low, slope_frame, m, bwd_send, bwd_recv, prev_sec) + (
            remote(cot.at[m], cot_in.at[m], bwd_send.at[m, 3], bwd_recv.at[m, 3], prev_sec, row),
        )

    @pl.loop(0, micro)
    def _(m):
        mid, down, up, whole = bwd_copies(m)

        @pl.when(last)
        def _():
            gap = output[m].astype(jnp.float32) - target[m].astype(jnp.float32)
            cot[m] = (gap * loss_scale).astype(jnp.bfloat16)

        @pl.when(sec < sections - 1)
        def _():
            mid.wait_recv()
            whole.wait_recv()

            @pl.when(has_low)
            def _():
                down.wait_recv()

            @pl.when(has_high)
            def _():
                up.wait_recv()

            pad[:, pl.ds(SIDE, breadth)] = slope_frame[m].astype(jnp.float32)

            @pl.loop(0, channels // LANES)
            def _(c):
                lanes = lanes_of(c)
                summed = jnp.zeros((height, breadth, LANES), jnp.float32)
                for b in range(KS):
                    column = columns(2 * MARGIN - b, lanes)
                    for a in range(KS):
                        begin = 2 * MARGIN - a
                        summed = (
                            summed
                            + taps_next[KS * a + b, :, lanes] * column[begin : begin + height]
                        )
                passed = cot_in[m, :, :, lanes].astype(jnp.float32) + summed
                cot[m, :, :, lanes] = passed.astype(jnp.bfloat16)

        arrived = cot[m].astype(jnp.float32).reshape(tokens, channels)
        small_sum[3] += eight_rows(arrived * branch_s[m])
        reduced = (arrived * scale[...]).astype(jnp.bfloat16)
        normal_slope = jnp.zeros((tokens, channels), jnp.float32)
        for f in range(hidden_units // piece):
            units = pl.ds(f * piece, piece)
            spread = contract_last(reduced, w_reduce[units, :])
            hidden_slope = (spread * bend_s[m, :, units]).astype(jnp.bfloat16)
            normal_slope = normal_slope + contract_last(hidden_slope, w_expand[:, units])
        normed = normed_s[m]
        scaled = normal_slope * gain[...]
        token_s[...] = normal_slope
        slope = (
            scaled
            - jnp.mean(scaled, axis=-1, keepdims=True)
            - normed * jnp.mean(scaled * normed, axis=-1, keepdims=True)
        ) * inverse_s[m][:, :1]
        slope_s[...] = slope.reshape(height, breadth, channels)

        @pl.when(sec > 0)
        def _():
            slope_low[m] = slope_s[...].astype(jnp.bfloat16)
            mid.start()
            whole.start()

            @pl.when(has_high)
            def _():
                down.start()

            @pl.when(has_low)
            def _():
                up.start()

        small_sum[0] += eight_rows(slope_s[...].reshape(tokens, channels))
        small_sum[1] += eight_rows(token_s[...] * normed_s[m])
        small_sum[2] += eight_rows(token_s[...])
        pad[:, pl.ds(SIDE, breadth)] = frame[m].astype(jnp.float32)

        @pl.loop(0, channels // LANES)
        def _(c):
            lanes = lanes_of(c)
            own = slope_s[:, :, lanes]
            for b in range(KS):
                column = columns(b, lanes)
                for a in range(KS):
                    term = (own * column[a : a + height]).reshape(tokens, LANES)
                    kernel_sum[KS * a + b, :, lanes] += eight_rows(term)

    spots = KS * KS
    share = parts.shape[1]
    for i in range(slabs * share):
        if i < spots:
            line = jnp.sum(kernel_sum[i], axis=0, keepdims=True)
        elif i < spots + 4:
            line = jnp.sum(small_sum[i - spots], axis=0, keepdims=True)
        else:
            line = jnp.zeros((1, channels), jnp.float32)
        parts[i // share, pl.ds(i % share, 1)] = line

    def sum_copy(other, arriving=False):
        at = other if arriving else row
        return remote(parts.at[other], slots.at[at], sum_send.at[other], sum_recv.at[at], sec, other)

    def whole_copy(other, arriving=False):
        at = other if arriving else row
        return remote(sums.at[at], sums.at[at], whole_send.at[other], whole_recv.at[at], sec, other)

    def each_other_slab(act):
        for other in range(slabs):
            @pl.when(row != other)
            def _(other=other):
                act(other)

    each_other_slab(lambda other: sum_copy(other).start())
    slots[row] = parts[row]
    each_other_slab(lambda other: sum_copy(other, True).wait_recv())
    total = slots[0]
    for other in range(1, slabs):
        total = total + slots[other]
    sums[row] = total
    each_other_slab(lambda other: whole_copy(other).start())
    each_other_slab(lambda other: whole_copy(other, True).wait_recv())
    small_outs = (offset_out, gain_out, shift_out, scale_out)
    for i in range(spots + 4):
        line = sums[i // share, pl.ds(i % share, 1)]
        if i < spots:
            kernel_out[i] = line
        else:
            small_outs[i - spots][...] = line

    if not gathered:
        finish_parts()
    each_other_slab(lambda other: sum_copy(other).wait_send())
    each_other_slab(lambda other: whole_copy(other).wait_send())

    @pl.when(sec > 0)
    def _():
        tap_copy.wait_send()

    @pl.loop(0, micro)
    def _(m):
        mid, down, up = fwd_copies(m)

        @pl.when(sec < sections - 1)
        def _():
            mid.wait_send()

            @pl.when(has_high)
            def _():
                down.wait_send()

            @pl.when(has_low)
            def _():
                up.wait_send()

        @pl.when(first)
        def _():
            _, edge_down, edge_up = edge_copies(m)

            @pl.when(has_high)
            def _():
                edge_down.wait_send()

            @pl.when(has_low)
            def _():
                edge_up.wait_send()

        mid, down, up, whole = bwd_copies(m)

        @pl.when(sec > 0)
        def _():
            mid.wait_send()
            whole.wait_send()

            @pl.when(has_high)
            def _():
                down.wait_send()

            @pl.when(has_low)
            def _():
                up.wait_send()


def per_device(
    latent, target, expand_weight, expand_bias, reduce_weight, reduce_bias,
    depth_kernel, depth_offset, norm_gain, norm_shift, layer_scale,
):
    sections, slabs = lax.axis_size("section"), lax.axis_size("rows")
    micro, height, breadth, channels = latent.shape
    hidden_units = expand_weight.shape[2]
    tokens = height * breadth
    tall = height + 2 * MARGIN
    spots = KS * KS
    share = -(-(spots + 4) // slabs)
    loss_scale = 1.0 / math.sqrt(micro * height * slabs * breadth)
    copies = lax.axis_size("groups")
    w_expand, w_reduce = expand_weight[0], reduce_weight[0]
    aligned = all(
        held.shape[0] % 16 == 0 and held.shape[1] % (LANES * copies) == 0
        for held in (w_expand, w_reduce)
    )
    if not aligned:
        w_expand = lax.all_gather(w_expand, "rows", axis=0, tiled=True)
        w_reduce = lax.all_gather(w_reduce, "rows", axis=0, tiled=True)
    low, wide = jnp.bfloat16, jnp.float32
    dma, vmem = pltpu.SemaphoreType.DMA, pltpu.VMEM
    found = pl.pallas_call(
        functools.partial(chain_kernel, sections, slabs, copies, not aligned, loss_scale),
        out_shape=(jax.ShapeDtypeStruct((spots, 1, channels), wide),)
        + (jax.ShapeDtypeStruct((1, channels), wide),) * 4,
        in_specs=[pl.BlockSpec(memory_space=pltpu.HBM)] * 11,
        out_specs=(pl.BlockSpec(memory_space=vmem),) * 5,
        scratch_shapes=[
            vmem(latent.shape, low), vmem(target.shape, low),
            vmem((channels, hidden_units), low), vmem((1, hidden_units), wide),
            vmem((hidden_units, channels), low), vmem((1, channels), wide),
            vmem((spots, 1, channels), wide),
            vmem((1, channels), wide), vmem((1, channels), wide),
            vmem((1, channels), wide), vmem((1, channels), wide),
            vmem((micro, tall, breadth, channels), low),
            vmem((micro, height, breadth, channels), low),
            vmem((micro, tokens, channels), wide),
            vmem((micro, tokens, LANES), wide),
            vmem((micro, tokens, hidden_units), wide),
            vmem((micro, tokens, channels), wide),
            vmem((micro, height, breadth, channels), low),
            vmem((micro, tall, breadth, channels), low),
            vmem((micro, height, breadth, channels), low),
            vmem((micro, height, breadth, channels), low),
            vmem((height, breadth, channels), wide),
            vmem((height, breadth, channels), wide),
            vmem((tokens, channels), wide),
            vmem((tall, breadth + 2 * SIDE, channels), wide),
            vmem((spots, 1, channels), wide),
            vmem((spots, 8, channels), wide),
            vmem((4, 8, channels), wide),
            vmem((slabs, share, channels), wide),
            vmem((slabs, share, channels), wide),
            vmem((slabs, share, channels), wide),
            dma((micro, 3)), dma((micro, 3)), dma((micro, 3)),
            dma((micro, 4)), dma((micro, 4)),
            dma, dma,
            dma((slabs,)), dma((slabs,)), dma((slabs,)), dma((slabs,)),
            dma((11,)), dma((2, slabs, 2 + copies)), dma((2, slabs, copies)),
        ],
        compiler_params=pltpu.CompilerParams(
            collective_id=0, has_side_effects=True, vmem_limit_bytes=62 * 1024 * 1024
        ),
        name="block_chain",
    )(
        latent, target, w_expand, expand_bias, w_reduce, reduce_bias,
        depth_kernel.transpose(1, 0, 2), depth_offset, norm_gain, norm_shift, layer_scale,
    )
    return (found[0].transpose(1, 0, 2),) + tuple(found[1:])


def solution(mesh):
    image = P("groups", "rows", None, None)
    matrix, vector = P("section", "rows", None), P("section", None)
    both = ("groups", "section")
    return jax.shard_map(
        per_device,
        mesh=mesh,
        in_specs=(
            image, image, matrix, vector, matrix, vector,
            P("section", None, None), vector, vector, vector, vector,
        ),
        out_specs=(P(both, None, None),) + (P(both, None),) * 4,
        check_vma=False,
    )
```

```python
import functools
import math

import jax
import jax.numpy as jnp
from jax import lax
from jax.experimental import pallas as pl
from jax.experimental.pallas import tpu as pltpu
from jax.sharding import PartitionSpec as P

KS = 7
MARGIN = KS // 2
LANES = 128
SIDE = 8
EPSILON = 1e-06
SQRT_HALF = 0.7071067811865476
INV_ROOT_TAU = 0.3989422804014327
MESH = pl.DeviceIdType.MESH
CUTS = 4


def contract_last(left, right):
    return lax.dot_general(
        left, right, (((1,), (1,)), ((), ())), preferred_element_type=jnp.float32
    )


def eight_rows(value):
    tokens, channels = value.shape
    return value.reshape(tokens // 8, 8, channels).sum(axis=0)


def chain_kernel(
    sections, slabs, copies, gathered, loss_scale,
    latent_in, target_in, w_expand_in, b_expand_in, w_reduce_in, b_reduce_in,
    taps_in, offset_in, gain_in, shift_in, scale_in,
    kernel_out, offset_out, gain_out, shift_out, scale_out,
    latent, target, w_expand, b_expand, w_reduce, b_reduce, taps, offset, gain, shift, scale,
    frame, output, normed_s, inverse_s, bend_s, branch_s,
    cot_in, slope_frame, cot, slope_low, slope_s, grid_s, token_s, pad, taps_next,
    kernel_sum, small_sum, parts, slots, sums,
    fwd_send, edge_send, fwd_recv, bwd_send, bwd_recv, tap_send, tap_recv, sum_send, sum_recv, whole_send, whole_recv,
    load_sem, part_send, part_recv,
):
    sec = lax.axis_index("section")
    row = lax.axis_index("rows")
    micro, height, breadth, channels = latent.shape
    tokens = height * breadth
    hidden_units = w_expand.shape[1]
    piece = 512 if hidden_units % 512 == 0 else LANES
    tall = height + 2 * MARGIN
    first, last = sec == 0, sec == sections - 1
    has_low, has_high = row > 0, row < slabs - 1

    group = lax.axis_index("groups")

    def rows_of(whole, shard):
        depth = whole.shape[0] // slabs
        return pl.ds(pl.multiple_of(shard * depth, 16), depth)

    local = []
    for source, dest in (
        (w_expand_in, w_expand), (w_reduce_in, w_reduce), (taps_in, taps), (latent_in, latent),
        (target_in, target), (b_expand_in, b_expand), (b_reduce_in, b_reduce),
        (offset_in, offset), (gain_in, gain), (shift_in, shift), (scale_in, scale),
    ):
        if len(local) < 2 and not gathered:
            dest = dest.at[rows_of(dest, row)]
        local.append(pltpu.make_async_copy(source, dest, load_sem.at[len(local)]))
        local[-1].start()

    barrier = pltpu.get_barrier_semaphore()
    greeted = jnp.int32(slabs - 1)
    for other in range(slabs):
        @pl.when(row != other)
        def _(other=other):
            pl.semaphore_signal(
                barrier, inc=1, device_id={"section": sec, "rows": other}, device_id_type=MESH
            )
    for ds in (-1, 1):
        for dr in (-1, 0, 1):
            there = (sec + ds >= 0) & (sec + ds < sections) & (row + dr >= 0) & (row + dr < slabs)

            @pl.when(there)
            def _(ds=ds, dr=dr):
                pl.semaphore_signal(
                    barrier, inc=1,
                    device_id={"section": sec + ds, "rows": row + dr}, device_id_type=MESH,
                )
            greeted = greeted + jnp.where(there, 1, 0)
    if not gathered:
        for other in range(copies):
            @pl.when(group != other)
            def _(other=other):
                pl.semaphore_signal(
                    barrier, inc=1, device_id={"groups": other}, device_id_type=MESH
                )
        greeted = greeted + (copies - 1)
    pl.semaphore_wait(barrier, greeted)

    weights = ((w_expand_in, w_expand),) * CUTS + ((w_reduce_in, w_reduce),) * CUTS

    def part_of(t, shard, part):
        whole = weights[t][1]
        depth, width = whole.shape[0] // slabs, whole.shape[1] // copies
        begin = shard * depth + (t % CUTS) * (depth // CUTS)
        return (
            pl.ds(pl.multiple_of(begin, 16), depth // CUTS),
            pl.ds(pl.multiple_of(part * width, LANES), width),
        )

    def along(t, shard, onward, own=False):
        rows, cols = part_of(t, shard, group)
        dest = weights[t][1].at[rows, cols]
        source = weights[t][0].at[part_of(t, 0, group)] if own else dest
        to_row = jnp.minimum(row + 1, slabs - 1) if onward == 0 else jnp.maximum(row - 1, 0)
        return pltpu.make_async_remote_copy(
            src_ref=source, dst_ref=dest,
            send_sem=part_send.at[t, shard, onward], recv_sem=part_recv.at[t, shard, group],
            device_id={"rows": to_row}, device_id_type=MESH,
        )

    def across(t, shard, other, arriving=False):
        part = other if arriving else group
        block = weights[t][1].at[part_of(t, shard, part)]
        return pltpu.make_async_remote_copy(
            src_ref=block, dst_ref=block,
            send_sem=part_send.at[t, shard, 2 + other], recv_sem=part_recv.at[t, shard, part],
            device_id={"groups": other}, device_id_type=MESH,
        )

    def each_other_copy(act):
        for other in range(copies):
            @pl.when(group != other)
            def _(other=other):
                act(other)

    def start_parts():
        for t in range(2 * CUTS):
            @pl.when(row < slabs - 1)
            def _(t=t):
                along(t, row, 0, own=True).start()

            @pl.when(row > 0)
            def _(t=t):
                along(t, row, 1, own=True).start()

    def pass_parts():
        for t in range(2 * CUTS):
            for far in range(1, slabs):
                @pl.when(row - far >= 0)
                def _(t=t, far=far):
                    shard = row - far
                    along(t, shard, 0).wait_recv()

                    @pl.when(row < slabs - 1)
                    def _():
                        along(t, shard, 0).start()
                    each_other_copy(lambda other: across(t, shard, other).start())

                @pl.when(row + far < slabs)
                def _(t=t, far=far):
                    shard = row + far
                    along(t, shard, 1).wait_recv()

                    @pl.when(row > 0)
                    def _():
                        along(t, shard, 1).start()
                    each_other_copy(lambda other: across(t, shard, other).start())
        for t in range(2 * CUTS):
            for shard in range(slabs):
                @pl.when(row != shard)
                def _(t=t, shard=shard):
                    each_other_copy(lambda other: across(t, shard, other, True).wait_recv())

    def finish_parts():
        for t in range(2 * CUTS):
            for shard in range(slabs):
                @pl.when((row >= shard) & (row < slabs - 1))
                def _(t=t, shard=shard):
                    along(t, shard, 0).wait_send()

                @pl.when((row <= shard) & (row > 0))
                def _(t=t, shard=shard):
                    along(t, shard, 1).wait_send()

                @pl.when(row != shard)
                def _(t=t, shard=shard):
                    each_other_copy(lambda other: across(t, shard, other).wait_send())

    if not gathered:
        start_parts()
    for copy in local:
        copy.wait()

    def remote(source, dest, send, recv, to_sec, to_row):
        return pltpu.make_async_remote_copy(
            src_ref=source, dst_ref=dest, send_sem=send, recv_sem=recv,
            device_id={"section": to_sec, "rows": to_row}, device_id_type=MESH,
        )

    def grid_copies(source, dest, m, send, recv, to_sec):
        low, high = jnp.maximum(row - 1, 0), jnp.minimum(row + 1, slabs - 1)
        return (
            remote(source.at[m], dest.at[m, pl.ds(MARGIN, height)],
                   send.at[m, 0], recv.at[m, 0], to_sec, row),
            remote(source.at[m, pl.ds(height - MARGIN, MARGIN)], dest.at[m, pl.ds(0, MARGIN)],
                   send.at[m, 1], recv.at[m, 1], to_sec, high),
            remote(source.at[m, pl.ds(0, MARGIN)], dest.at[m, pl.ds(MARGIN + height, MARGIN)],
                   send.at[m, 2], recv.at[m, 2], to_sec, low),
        )

    def fwd_copies(m):
        return grid_copies(output, frame, m, fwd_send, fwd_recv, next_sec)

    def edge_copies(m):
        return grid_copies(latent, frame, m, edge_send, fwd_recv, sec)

    next_sec = jnp.minimum(sec + 1, sections - 1)
    prev_sec = jnp.maximum(sec - 1, 0)
    tap_copy = remote(taps, taps_next, tap_send, tap_recv, prev_sec, row)

    @pl.when(sec > 0)
    def _():
        tap_copy.start()

    @pl.when(first)
    def _():
        for m in range(micro):
            _, down, up = edge_copies(m)

            @pl.when(has_high)
            def _():
                down.start()

            @pl.when(has_low)
            def _():
                up.start()
            frame[m, pl.ds(MARGIN, height)] = latent[m]

    edge = jnp.zeros((micro, MARGIN, breadth, channels), jnp.bfloat16)

    @pl.when(row == 0)
    def _():
        frame[:, pl.ds(0, MARGIN)] = edge
        slope_frame[:, pl.ds(0, MARGIN)] = edge

    @pl.when(row == slabs - 1)
    def _():
        frame[:, pl.ds(MARGIN + height, MARGIN)] = edge
        slope_frame[:, pl.ds(MARGIN + height, MARGIN)] = edge

    pad[:, pl.ds(0, SIDE)] = jnp.zeros((tall, SIDE, channels), jnp.float32)
    pad[:, pl.ds(SIDE + breadth, SIDE)] = jnp.zeros((tall, SIDE, channels), jnp.float32)
    kernel_sum[...] = jnp.zeros_like(kernel_sum)
    small_sum[...] = jnp.zeros_like(small_sum)
    if not gathered:
        pass_parts()

    def lanes_of(c):
        return pl.ds(pl.multiple_of(c * LANES, LANES), LANES)

    def columns(col_off, lanes):
        return pad[:, pl.ds(SIDE - MARGIN + col_off, breadth), lanes]

    @pl.loop(0, micro)
    def _(m):
        mid, down, up = fwd_copies(m)

        @pl.when(sec > 0)
        def _():
            mid.wait_recv()

        @pl.when(has_low)
        def _():
            down.wait_recv()

        @pl.when(has_high)
        def _():
            up.wait_recv()

        pad[:, pl.ds(SIDE, breadth)] = frame[m].astype(jnp.float32)

        @pl.loop(0, channels // LANES)
        def _(c):
            lanes = lanes_of(c)
            summed = jnp.zeros((height, breadth, LANES), jnp.float32) + offset[:, lanes]
            for b in range(KS):
                column = columns(b, lanes)
                for a in range(KS):
                    summed = summed + taps[KS * a + b, :, lanes] * column[a : a + height]
            grid_s[:, :, lanes] = summed

        mixed = grid_s[...].reshape(tokens, channels)
        centred = mixed - jnp.mean(mixed, axis=-1, keepdims=True)
        variance = jnp.mean(centred * centred, axis=-1, keepdims=True)
        inverse = lax.rsqrt(variance + EPSILON)
        normed = centred * inverse
        normed_s[m] = normed
        inverse_s[m] = jnp.broadcast_to(inverse, (tokens, LANES))
        inputs = (normed * gain[...] + shift[...]).astype(jnp.bfloat16)
        branch = jnp.zeros((tokens, channels), jnp.float32) + b_reduce[...]
        for f in range(hidden_units // piece):
            units = pl.ds(f * piece, piece)
            hidden = (
                jnp.dot(inputs, w_expand[:, units], preferred_element_type=jnp.float32)
                + b_expand[:, units]
            )
            below = 0.5 * (1.0 + lax.erf(hidden * SQRT_HALF))
            bend_s[m, :, units] = below + hidden * jnp.exp(-0.5 * hidden * hidden) * INV_ROOT_TAU
            active = (hidden * below).astype(jnp.bfloat16)
            branch = branch + jnp.dot(active, w_reduce[units, :], preferred_element_type=jnp.float32)
        branch_s[m] = branch
        source = frame[m, pl.ds(MARGIN, height)].astype(jnp.float32)
        grown = source + (scale[...] * branch).reshape(height, breadth, channels)
        output[m] = grown.astype(jnp.bfloat16)

        @pl.when(sec < sections - 1)
        def _():
            mid.start()

            @pl.when(has_high)
            def _():
                down.start()

            @pl.when(has_low)
            def _():
                up.start()

    @pl.when(sec < sections - 1)
    def _():
        tap_copy.wait_recv()

    def bwd_copies(m):
        return grid_copies(slope_low, slope_frame, m, bwd_send, bwd_recv, prev_sec) + (
            remote(cot.at[m], cot_in.at[m], bwd_send.at[m, 3], bwd_recv.at[m, 3], prev_sec, row),
        )

    @pl.loop(0, micro)
    def _(m):
        mid, down, up, whole = bwd_copies(m)

        @pl.when(last)
        def _():
            gap = output[m].astype(jnp.float32) - target[m].astype(jnp.float32)
            cot[m] = (gap * loss_scale).astype(jnp.bfloat16)

        @pl.when(sec < sections - 1)
        def _():
            mid.wait_recv()
            whole.wait_recv()

            @pl.when(has_low)
            def _():
                down.wait_recv()

            @pl.when(has_high)
            def _():
                up.wait_recv()

            pad[:, pl.ds(SIDE, breadth)] = slope_frame[m].astype(jnp.float32)

            @pl.loop(0, channels // LANES)
            def _(c):
                lanes = lanes_of(c)
                summed = jnp.zeros((height, breadth, LANES), jnp.float32)
                for b in range(KS):
                    column = columns(2 * MARGIN - b, lanes)
                    for a in range(KS):
                        begin = 2 * MARGIN - a
                        summed = (
                            summed
                            + taps_next[KS * a + b, :, lanes] * column[begin : begin + height]
                        )
                passed = cot_in[m, :, :, lanes].astype(jnp.float32) + summed
                cot[m, :, :, lanes] = passed.astype(jnp.bfloat16)

        arrived = cot[m].astype(jnp.float32).reshape(tokens, channels)
        small_sum[3] += eight_rows(arrived * branch_s[m])
        reduced = (arrived * scale[...]).astype(jnp.bfloat16)
        normal_slope = jnp.zeros((tokens, channels), jnp.float32)
        for f in range(hidden_units // piece):
            units = pl.ds(f * piece, piece)
            spread = contract_last(reduced, w_reduce[units, :])
            hidden_slope = (spread * bend_s[m, :, units]).astype(jnp.bfloat16)
            normal_slope = normal_slope + contract_last(hidden_slope, w_expand[:, units])
        normed = normed_s[m]
        scaled = normal_slope * gain[...]
        token_s[...] = normal_slope
        slope = (
            scaled
            - jnp.mean(scaled, axis=-1, keepdims=True)
            - normed * jnp.mean(scaled * normed, axis=-1, keepdims=True)
        ) * inverse_s[m][:, :1]
        slope_s[...] = slope.reshape(height, breadth, channels)

        @pl.when(sec > 0)
        def _():
            slope_low[m] = slope_s[...].astype(jnp.bfloat16)
            mid.start()
            whole.start()

            @pl.when(has_high)
            def _():
                down.start()

            @pl.when(has_low)
            def _():
                up.start()

        small_sum[0] += eight_rows(slope_s[...].reshape(tokens, channels))
        small_sum[1] += eight_rows(token_s[...] * normed_s[m])
        small_sum[2] += eight_rows(token_s[...])
        pad[:, pl.ds(SIDE, breadth)] = frame[m].astype(jnp.float32)

        @pl.loop(0, channels // LANES)
        def _(c):
            lanes = lanes_of(c)
            own = slope_s[:, :, lanes]
            for b in range(KS):
                column = columns(b, lanes)
                for a in range(KS):
                    term = (own * column[a : a + height]).reshape(tokens, LANES)
                    kernel_sum[KS * a + b, :, lanes] += eight_rows(term)

    spots = KS * KS
    share = parts.shape[1]
    for i in range(slabs * share):
        if i < spots:
            line = jnp.sum(kernel_sum[i], axis=0, keepdims=True)
        elif i < spots + 4:
            line = jnp.sum(small_sum[i - spots], axis=0, keepdims=True)
        else:
            line = jnp.zeros((1, channels), jnp.float32)
        parts[i // share, pl.ds(i % share, 1)] = line

    def sum_copy(other, arriving=False):
        at = other if arriving else row
        return remote(parts.at[other], slots.at[at], sum_send.at[other], sum_recv.at[at], sec, other)

    def whole_copy(other, arriving=False):
        at = other if arriving else row
        return remote(sums.at[at], sums.at[at], whole_send.at[other], whole_recv.at[at], sec, other)

    def each_other_slab(act):
        for other in range(slabs):
            @pl.when(row != other)
            def _(other=other):
                act(other)

    each_other_slab(lambda other: sum_copy(other).start())
    slots[row] = parts[row]
    each_other_slab(lambda other: sum_copy(other, True).wait_recv())
    total = slots[0]
    for other in range(1, slabs):
        total = total + slots[other]
    sums[row] = total
    each_other_slab(lambda other: whole_copy(other).start())
    each_other_slab(lambda other: whole_copy(other, True).wait_recv())
    small_outs = (offset_out, gain_out, shift_out, scale_out)
    for i in range(spots + 4):
        line = sums[i // share, pl.ds(i % share, 1)]
        if i < spots:
            kernel_out[i] = line
        else:
            small_outs[i - spots][...] = line

    if not gathered:
        finish_parts()
    each_other_slab(lambda other: sum_copy(other).wait_send())
    each_other_slab(lambda other: whole_copy(other).wait_send())

    @pl.when(sec > 0)
    def _():
        tap_copy.wait_send()

    @pl.loop(0, micro)
    def _(m):
        mid, down, up = fwd_copies(m)

        @pl.when(sec < sections - 1)
        def _():
            mid.wait_send()

            @pl.when(has_high)
            def _():
                down.wait_send()

            @pl.when(has_low)
            def _():
                up.wait_send()

        @pl.when(first)
        def _():
            _, edge_down, edge_up = edge_copies(m)

            @pl.when(has_high)
            def _():
                edge_down.wait_send()

            @pl.when(has_low)
            def _():
                edge_up.wait_send()

        mid, down, up, whole = bwd_copies(m)

        @pl.when(sec > 0)
        def _():
            mid.wait_send()
            whole.wait_send()

            @pl.when(has_high)
            def _():
                down.wait_send()

            @pl.when(has_low)
            def _():
                up.wait_send()


def per_device(
    latent, target, expand_weight, expand_bias, reduce_weight, reduce_bias,
    depth_kernel, depth_offset, norm_gain, norm_shift, layer_scale,
):
    sections, slabs = lax.axis_size("section"), lax.axis_size("rows")
    micro, height, breadth, channels = latent.shape
    hidden_units = expand_weight.shape[2]
    tokens = height * breadth
    tall = height + 2 * MARGIN
    spots = KS * KS
    share = -(-(spots + 4) // slabs)
    loss_scale = 1.0 / math.sqrt(micro * height * slabs * breadth)
    copies = lax.axis_size("groups")
    w_expand, w_reduce = expand_weight[0], reduce_weight[0]
    aligned = all(
        held.shape[0] % (16 * CUTS) == 0 and held.shape[1] % (LANES * copies) == 0
        for held in (w_expand, w_reduce)
    )
    if not aligned:
        w_expand = lax.all_gather(w_expand, "rows", axis=0, tiled=True)
        w_reduce = lax.all_gather(w_reduce, "rows", axis=0, tiled=True)
    low, wide = jnp.bfloat16, jnp.float32
    dma, vmem = pltpu.SemaphoreType.DMA, pltpu.VMEM
    found = pl.pallas_call(
        functools.partial(chain_kernel, sections, slabs, copies, not aligned, loss_scale),
        out_shape=(jax.ShapeDtypeStruct((spots, 1, channels), wide),)
        + (jax.ShapeDtypeStruct((1, channels), wide),) * 4,
        in_specs=[pl.BlockSpec(memory_space=pltpu.HBM)] * 11,
        out_specs=(pl.BlockSpec(memory_space=vmem),) * 5,
        scratch_shapes=[
            vmem(latent.shape, low), vmem(target.shape, low),
            vmem((channels, hidden_units), low), vmem((1, hidden_units), wide),
            vmem((hidden_units, channels), low), vmem((1, channels), wide),
            vmem((spots, 1, channels), wide),
            vmem((1, channels), wide), vmem((1, channels), wide),
            vmem((1, channels), wide), vmem((1, channels), wide),
            vmem((micro, tall, breadth, channels), low),
            vmem((micro, height, breadth, channels), low),
            vmem((micro, tokens, channels), wide),
            vmem((micro, tokens, LANES), wide),
            vmem((micro, tokens, hidden_units), wide),
            vmem((micro, tokens, channels), wide),
            vmem((micro, height, breadth, channels), low),
            vmem((micro, tall, breadth, channels), low),
            vmem((micro, height, breadth, channels), low),
            vmem((micro, height, breadth, channels), low),
            vmem((height, breadth, channels), wide),
            vmem((height, breadth, channels), wide),
            vmem((tokens, channels), wide),
            vmem((tall, breadth + 2 * SIDE, channels), wide),
            vmem((spots, 1, channels), wide),
            vmem((spots, 8, channels), wide),
            vmem((4, 8, channels), wide),
            vmem((slabs, share, channels), wide),
            vmem((slabs, share, channels), wide),
            vmem((slabs, share, channels), wide),
            dma((micro, 3)), dma((micro, 3)), dma((micro, 3)),
            dma((micro, 4)), dma((micro, 4)),
            dma, dma,
            dma((slabs,)), dma((slabs,)), dma((slabs,)), dma((slabs,)),
            dma((11,)), dma((2 * CUTS, slabs, 2 + copies)),
            dma((2 * CUTS, slabs, copies)),
        ],
        compiler_params=pltpu.CompilerParams(
            collective_id=0, has_side_effects=True, vmem_limit_bytes=62 * 1024 * 1024
        ),
        name="block_chain",
    )(
        latent, target, w_expand, expand_bias, w_reduce, reduce_bias,
        depth_kernel.transpose(1, 0, 2), depth_offset, norm_gain, norm_shift, layer_scale,
    )
    return (found[0].transpose(1, 0, 2),) + tuple(found[1:])


def solution(mesh):
    image = P("groups", "rows", None, None)
    matrix, vector = P("section", "rows", None), P("section", None)
    both = ("groups", "section")
    return jax.shard_map(
        per_device,
        mesh=mesh,
        in_specs=(
            image, image, matrix, vector, matrix, vector,
            P("section", None, None), vector, vector, vector, vector,
        ),
        out_specs=(P(both, None, None),) + (P(both, None),) * 4,
        check_vma=False,
    )
```

```python
import functools
import math

import jax
import jax.numpy as jnp
from jax import lax
from jax.experimental import pallas as pl
from jax.experimental.pallas import tpu as pltpu
from jax.sharding import PartitionSpec as P

KS = 7
MARGIN = KS // 2
LANES = 128
SIDE = 8
EPSILON = 1e-06
SQRT_HALF = 0.7071067811865476
INV_ROOT_TAU = 0.3989422804014327
MESH = pl.DeviceIdType.MESH


def contract_last(left, right):
    return lax.dot_general(
        left, right, (((1,), (1,)), ((), ())), preferred_element_type=jnp.float32
    )


def eight_rows(value):
    tokens, channels = value.shape
    return value.reshape(tokens // 8, 8, channels).sum(axis=0)


def chain_kernel(
    sections, slabs, copies, gathered, loss_scale,
    latent_in, target_in, w_expand_in, b_expand_in, w_reduce_in, b_reduce_in,
    taps_in, offset_in, gain_in, shift_in, scale_in,
    kernel_out, offset_out, gain_out, shift_out, scale_out,
    latent, target, w_expand, b_expand, w_reduce, b_reduce, taps, offset, gain, shift, scale,
    frame, output, normed_s, inverse_s, bend_s, branch_s,
    cot_in, slope_frame, cot, slope_low, slope_s, grid_s, token_s, pad, taps_next,
    kernel_sum, small_sum, parts, slots, sums,
    fwd_send, edge_send, fwd_recv, bwd_send, bwd_recv, tap_send, tap_recv, sum_send, sum_recv, whole_send, whole_recv,
    load_sem, part_send, part_recv,
):
    sec = lax.axis_index("section")
    row = lax.axis_index("rows")
    micro, height, breadth, channels = latent.shape
    tokens = height * breadth
    hidden_units = w_expand.shape[1]
    piece = 512 if hidden_units % 512 == 0 else LANES
    tall = height + 2 * MARGIN
    first, last = sec == 0, sec == sections - 1
    has_low, has_high = row > 0, row < slabs - 1

    group = lax.axis_index("groups")

    def rows_of(whole, shard):
        depth = whole.shape[0] // slabs
        return pl.ds(pl.multiple_of(shard * depth, 16), depth)

    local = []
    for source, dest in (
        (w_expand_in, w_expand), (w_reduce_in, w_reduce), (taps_in, taps), (latent_in, latent),
        (target_in, target), (b_expand_in, b_expand), (b_reduce_in, b_reduce),
        (offset_in, offset), (gain_in, gain), (shift_in, shift), (scale_in, scale),
    ):
        if len(local) < 2 and not gathered:
            dest = dest.at[rows_of(dest, row)]
        local.append(pltpu.make_async_copy(source, dest, load_sem.at[len(local)]))
        local[-1].start()

    barrier = pltpu.get_barrier_semaphore()
    greeted = jnp.int32(slabs - 1)
    for other in range(slabs):
        @pl.when(row != other)
        def _(other=other):
            pl.semaphore_signal(
                barrier, inc=1, device_id={"section": sec, "rows": other}, device_id_type=MESH
            )
    for ds in (-1, 1):
        for dr in (-1, 0, 1):
            there = (sec + ds >= 0) & (sec + ds < sections) & (row + dr >= 0) & (row + dr < slabs)

            @pl.when(there)
            def _(ds=ds, dr=dr):
                pl.semaphore_signal(
                    barrier, inc=1,
                    device_id={"section": sec + ds, "rows": row + dr}, device_id_type=MESH,
                )
            greeted = greeted + jnp.where(there, 1, 0)
    if not gathered:
        for other in range(copies):
            @pl.when(group != other)
            def _(other=other):
                pl.semaphore_signal(
                    barrier, inc=1, device_id={"groups": other}, device_id_type=MESH
                )
        greeted = greeted + (copies - 1)
    pl.semaphore_wait(barrier, greeted)

    weights = ((w_expand_in, w_expand), (w_reduce_in, w_reduce))

    def part_of(t, shard, part):
        width = weights[t][1].shape[1] // copies
        return rows_of(weights[t][1], shard), pl.ds(pl.multiple_of(part * width, LANES), width)

    def along(t, shard, onward, own=False):
        rows, cols = part_of(t, shard, group)
        dest = weights[t][1].at[rows, cols]
        source = weights[t][0].at[:, cols] if own else dest
        to_row = jnp.minimum(row + 1, slabs - 1) if onward == 0 else jnp.maximum(row - 1, 0)
        return pltpu.make_async_remote_copy(
            src_ref=source, dst_ref=dest,
            send_sem=part_send.at[t, shard, onward], recv_sem=part_recv.at[t, shard, group],
            device_id={"rows": to_row}, device_id_type=MESH,
        )

    def across(t, shard, other, arriving=False):
        part = other if arriving else group
        block = weights[t][1].at[part_of(t, shard, part)]
        return pltpu.make_async_remote_copy(
            src_ref=block, dst_ref=block,
            send_sem=part_send.at[t, shard, 2 + other], recv_sem=part_recv.at[t, shard, part],
            device_id={"groups": other}, device_id_type=MESH,
        )

    def each_other_copy(act):
        for other in range(copies):
            @pl.when(group != other)
            def _(other=other):
                act(other)

    def start_parts():
        for t in range(2):
            @pl.when(row < slabs - 1)
            def _(t=t):
                along(t, row, 0, own=True).start()

            @pl.when(row > 0)
            def _(t=t):
                along(t, row, 1, own=True).start()

    def pass_parts():
        for t in range(2):
            for far in range(1, slabs):
                @pl.when(row - far >= 0)
                def _(t=t, far=far):
                    shard = row - far
                    along(t, shard, 0).wait_recv()

                    @pl.when(row < slabs - 1)
                    def _():
                        along(t, shard, 0).start()
                    each_other_copy(lambda other: across(t, shard, other).start())

                @pl.when(row + far < slabs)
                def _(t=t, far=far):
                    shard = row + far
                    along(t, shard, 1).wait_recv()

                    @pl.when(row > 0)
                    def _():
                        along(t, shard, 1).start()
                    each_other_copy(lambda other: across(t, shard, other).start())

    def take_parts(t, m):
        if gathered:
            return
        for shard in range(slabs):
            @pl.when((m == 0) & (row != shard))
            def _(shard=shard):
                each_other_copy(lambda other: across(t, shard, other, True).wait_recv())

    def finish_parts():
        for t in range(2):
            for shard in range(slabs):
                @pl.when((row >= shard) & (row < slabs - 1))
                def _(t=t, shard=shard):
                    along(t, shard, 0).wait_send()

                @pl.when((row <= shard) & (row > 0))
                def _(t=t, shard=shard):
                    along(t, shard, 1).wait_send()

                @pl.when(row != shard)
                def _(t=t, shard=shard):
                    each_other_copy(lambda other: across(t, shard, other).wait_send())

    if not gathered:
        start_parts()
    for copy in local:
        copy.wait()

    def remote(source, dest, send, recv, to_sec, to_row):
        return pltpu.make_async_remote_copy(
            src_ref=source, dst_ref=dest, send_sem=send, recv_sem=recv,
            device_id={"section": to_sec, "rows": to_row}, device_id_type=MESH,
        )

    def grid_copies(source, dest, m, send, recv, to_sec):
        low, high = jnp.maximum(row - 1, 0), jnp.minimum(row + 1, slabs - 1)
        return (
            remote(source.at[m], dest.at[m, pl.ds(MARGIN, height)],
                   send.at[m, 0], recv.at[m, 0], to_sec, row),
            remote(source.at[m, pl.ds(height - MARGIN, MARGIN)], dest.at[m, pl.ds(0, MARGIN)],
                   send.at[m, 1], recv.at[m, 1], to_sec, high),
            remote(source.at[m, pl.ds(0, MARGIN)], dest.at[m, pl.ds(MARGIN + height, MARGIN)],
                   send.at[m, 2], recv.at[m, 2], to_sec, low),
        )

    def fwd_copies(m):
        return grid_copies(output, frame, m, fwd_send, fwd_recv, next_sec)

    def edge_copies(m):
        return grid_copies(latent, frame, m, edge_send, fwd_recv, sec)

    next_sec = jnp.minimum(sec + 1, sections - 1)
    prev_sec = jnp.maximum(sec - 1, 0)
    tap_copy = remote(taps, taps_next, tap_send, tap_recv, prev_sec, row)

    @pl.when(sec > 0)
    def _():
        tap_copy.start()

    @pl.when(first)
    def _():
        for m in range(micro):
            _, down, up = edge_copies(m)

            @pl.when(has_high)
            def _():
                down.start()

            @pl.when(has_low)
            def _():
                up.start()
            frame[m, pl.ds(MARGIN, height)] = latent[m]

    edge = jnp.zeros((micro, MARGIN, breadth, channels), jnp.bfloat16)

    @pl.when(row == 0)
    def _():
        frame[:, pl.ds(0, MARGIN)] = edge
        slope_frame[:, pl.ds(0, MARGIN)] = edge

    @pl.when(row == slabs - 1)
    def _():
        frame[:, pl.ds(MARGIN + height, MARGIN)] = edge
        slope_frame[:, pl.ds(MARGIN + height, MARGIN)] = edge

    pad[:, pl.ds(0, SIDE)] = jnp.zeros((tall, SIDE, channels), jnp.float32)
    pad[:, pl.ds(SIDE + breadth, SIDE)] = jnp.zeros((tall, SIDE, channels), jnp.float32)
    kernel_sum[...] = jnp.zeros_like(kernel_sum)
    small_sum[...] = jnp.zeros_like(small_sum)
    if not gathered:
        pass_parts()

    def lanes_of(c):
        return pl.ds(pl.multiple_of(c * LANES, LANES), LANES)

    def columns(col_off, lanes):
        return pad[:, pl.ds(SIDE - MARGIN + col_off, breadth), lanes]

    @pl.loop(0, micro)
    def _(m):
        mid, down, up = fwd_copies(m)

        @pl.when(sec > 0)
        def _():
            mid.wait_recv()

        @pl.when(has_low)
        def _():
            down.wait_recv()

        @pl.when(has_high)
        def _():
            up.wait_recv()

        pad[:, pl.ds(SIDE, breadth)] = frame[m].astype(jnp.float32)

        @pl.loop(0, channels // LANES)
        def _(c):
            lanes = lanes_of(c)
            summed = jnp.zeros((height, breadth, LANES), jnp.float32) + offset[:, lanes]
            for b in range(KS):
                column = columns(b, lanes)
                for a in range(KS):
                    summed = summed + taps[KS * a + b, :, lanes] * column[a : a + height]
            grid_s[:, :, lanes] = summed

        mixed = grid_s[...].reshape(tokens, channels)
        centred = mixed - jnp.mean(mixed, axis=-1, keepdims=True)
        variance = jnp.mean(centred * centred, axis=-1, keepdims=True)
        inverse = lax.rsqrt(variance + EPSILON)
        normed = centred * inverse
        normed_s[m] = normed
        inverse_s[m] = jnp.broadcast_to(inverse, (tokens, LANES))
        inputs = (normed * gain[...] + shift[...]).astype(jnp.bfloat16)
        branch = jnp.zeros((tokens, channels), jnp.float32) + b_reduce[...]
        take_parts(0, m)
        for f in range(hidden_units // piece):
            units = pl.ds(f * piece, piece)
            hidden = (
                jnp.dot(inputs, w_expand[:, units], preferred_element_type=jnp.float32)
                + b_expand[:, units]
            )
            below = 0.5 * (1.0 + lax.erf(hidden * SQRT_HALF))
            bend_s[m, :, units] = below + hidden * jnp.exp(-0.5 * hidden * hidden) * INV_ROOT_TAU
            active = (hidden * below).astype(jnp.bfloat16)
            if f == 0:
                take_parts(1, m)
            branch = branch + jnp.dot(active, w_reduce[units, :], preferred_element_type=jnp.float32)
        branch_s[m] = branch
        source = frame[m, pl.ds(MARGIN, height)].astype(jnp.float32)
        grown = source + (scale[...] * branch).reshape(height, breadth, channels)
        output[m] = grown.astype(jnp.bfloat16)

        @pl.when(sec < sections - 1)
        def _():
            mid.start()

            @pl.when(has_high)
            def _():
                down.start()

            @pl.when(has_low)
            def _():
                up.start()

    @pl.when(sec < sections - 1)
    def _():
        tap_copy.wait_recv()

    def bwd_copies(m):
        return grid_copies(slope_low, slope_frame, m, bwd_send, bwd_recv, prev_sec) + (
            remote(cot.at[m], cot_in.at[m], bwd_send.at[m, 3], bwd_recv.at[m, 3], prev_sec, row),
        )

    @pl.loop(0, micro)
    def _(m):
        mid, down, up, whole = bwd_copies(m)

        @pl.when(last)
        def _():
            gap = output[m].astype(jnp.float32) - target[m].astype(jnp.float32)
            cot[m] = (gap * loss_scale).astype(jnp.bfloat16)

        @pl.when(sec < sections - 1)
        def _():
            mid.wait_recv()
            whole.wait_recv()

            @pl.when(has_low)
            def _():
                down.wait_recv()

            @pl.when(has_high)
            def _():
                up.wait_recv()

            pad[:, pl.ds(SIDE, breadth)] = slope_frame[m].astype(jnp.float32)

            @pl.loop(0, channels // LANES)
            def _(c):
                lanes = lanes_of(c)
                summed = jnp.zeros((height, breadth, LANES), jnp.float32)
                for b in range(KS):
                    column = columns(2 * MARGIN - b, lanes)
                    for a in range(KS):
                        begin = 2 * MARGIN - a
                        summed = (
                            summed
                            + taps_next[KS * a + b, :, lanes] * column[begin : begin + height]
                        )
                passed = cot_in[m, :, :, lanes].astype(jnp.float32) + summed
                cot[m, :, :, lanes] = passed.astype(jnp.bfloat16)

        arrived = cot[m].astype(jnp.float32).reshape(tokens, channels)
        small_sum[3] += eight_rows(arrived * branch_s[m])
        reduced = (arrived * scale[...]).astype(jnp.bfloat16)
        normal_slope = jnp.zeros((tokens, channels), jnp.float32)
        for f in range(hidden_units // piece):
            units = pl.ds(f * piece, piece)
            spread = contract_last(reduced, w_reduce[units, :])
            hidden_slope = (spread * bend_s[m, :, units]).astype(jnp.bfloat16)
            normal_slope = normal_slope + contract_last(hidden_slope, w_expand[:, units])
        normed = normed_s[m]
        scaled = normal_slope * gain[...]
        token_s[...] = normal_slope
        slope = (
            scaled
            - jnp.mean(scaled, axis=-1, keepdims=True)
            - normed * jnp.mean(scaled * normed, axis=-1, keepdims=True)
        ) * inverse_s[m][:, :1]
        slope_s[...] = slope.reshape(height, breadth, channels)

        @pl.when(sec > 0)
        def _():
            slope_low[m] = slope_s[...].astype(jnp.bfloat16)
            mid.start()
            whole.start()

            @pl.when(has_high)
            def _():
                down.start()

            @pl.when(has_low)
            def _():
                up.start()

        small_sum[0] += eight_rows(slope_s[...].reshape(tokens, channels))
        small_sum[1] += eight_rows(token_s[...] * normed_s[m])
        small_sum[2] += eight_rows(token_s[...])
        pad[:, pl.ds(SIDE, breadth)] = frame[m].astype(jnp.float32)

        @pl.loop(0, channels // LANES)
        def _(c):
            lanes = lanes_of(c)
            own = slope_s[:, :, lanes]
            for b in range(KS):
                column = columns(b, lanes)
                for a in range(KS):
                    term = (own * column[a : a + height]).reshape(tokens, LANES)
                    kernel_sum[KS * a + b, :, lanes] += eight_rows(term)

    spots = KS * KS
    share = parts.shape[1]
    for i in range(slabs * share):
        if i < spots:
            line = jnp.sum(kernel_sum[i], axis=0, keepdims=True)
        elif i < spots + 4:
            line = jnp.sum(small_sum[i - spots], axis=0, keepdims=True)
        else:
            line = jnp.zeros((1, channels), jnp.float32)
        parts[i // share, pl.ds(i % share, 1)] = line

    def sum_copy(other, arriving=False):
        at = other if arriving else row
        return remote(parts.at[other], slots.at[at], sum_send.at[other], sum_recv.at[at], sec, other)

    def whole_copy(other, arriving=False):
        at = other if arriving else row
        return remote(sums.at[at], sums.at[at], whole_send.at[other], whole_recv.at[at], sec, other)

    def each_other_slab(act):
        for other in range(slabs):
            @pl.when(row != other)
            def _(other=other):
                act(other)

    each_other_slab(lambda other: sum_copy(other).start())
    slots[row] = parts[row]
    each_other_slab(lambda other: sum_copy(other, True).wait_recv())
    total = slots[0]
    for other in range(1, slabs):
        total = total + slots[other]
    sums[row] = total
    each_other_slab(lambda other: whole_copy(other).start())
    each_other_slab(lambda other: whole_copy(other, True).wait_recv())
    small_outs = (offset_out, gain_out, shift_out, scale_out)
    for i in range(spots + 4):
        line = sums[i // share, pl.ds(i % share, 1)]
        if i < spots:
            kernel_out[i] = line
        else:
            small_outs[i - spots][...] = line

    if not gathered:
        finish_parts()
    each_other_slab(lambda other: sum_copy(other).wait_send())
    each_other_slab(lambda other: whole_copy(other).wait_send())

    @pl.when(sec > 0)
    def _():
        tap_copy.wait_send()

    @pl.loop(0, micro)
    def _(m):
        mid, down, up = fwd_copies(m)

        @pl.when(sec < sections - 1)
        def _():
            mid.wait_send()

            @pl.when(has_high)
            def _():
                down.wait_send()

            @pl.when(has_low)
            def _():
                up.wait_send()

        @pl.when(first)
        def _():
            _, edge_down, edge_up = edge_copies(m)

            @pl.when(has_high)
            def _():
                edge_down.wait_send()

            @pl.when(has_low)
            def _():
                edge_up.wait_send()

        mid, down, up, whole = bwd_copies(m)

        @pl.when(sec > 0)
        def _():
            mid.wait_send()
            whole.wait_send()

            @pl.when(has_high)
            def _():
                down.wait_send()

            @pl.when(has_low)
            def _():
                up.wait_send()


def per_device(
    latent, target, expand_weight, expand_bias, reduce_weight, reduce_bias,
    depth_kernel, depth_offset, norm_gain, norm_shift, layer_scale,
):
    sections, slabs = lax.axis_size("section"), lax.axis_size("rows")
    micro, height, breadth, channels = latent.shape
    hidden_units = expand_weight.shape[2]
    tokens = height * breadth
    tall = height + 2 * MARGIN
    spots = KS * KS
    share = -(-(spots + 4) // slabs)
    loss_scale = 1.0 / math.sqrt(micro * height * slabs * breadth)
    copies = lax.axis_size("groups")
    w_expand, w_reduce = expand_weight[0], reduce_weight[0]
    aligned = all(
        held.shape[0] % 16 == 0 and held.shape[1] % (LANES * copies) == 0
        for held in (w_expand, w_reduce)
    )
    if not aligned:
        w_expand = lax.all_gather(w_expand, "rows", axis=0, tiled=True)
        w_reduce = lax.all_gather(w_reduce, "rows", axis=0, tiled=True)
    low, wide = jnp.bfloat16, jnp.float32
    dma, vmem = pltpu.SemaphoreType.DMA, pltpu.VMEM
    found = pl.pallas_call(
        functools.partial(chain_kernel, sections, slabs, copies, not aligned, loss_scale),
        out_shape=(jax.ShapeDtypeStruct((spots, 1, channels), wide),)
        + (jax.ShapeDtypeStruct((1, channels), wide),) * 4,
        in_specs=[pl.BlockSpec(memory_space=pltpu.HBM)] * 11,
        out_specs=(pl.BlockSpec(memory_space=vmem),) * 5,
        scratch_shapes=[
            vmem(latent.shape, low), vmem(target.shape, low),
            vmem((channels, hidden_units), low), vmem((1, hidden_units), wide),
            vmem((hidden_units, channels), low), vmem((1, channels), wide),
            vmem((spots, 1, channels), wide),
            vmem((1, channels), wide), vmem((1, channels), wide),
            vmem((1, channels), wide), vmem((1, channels), wide),
            vmem((micro, tall, breadth, channels), low),
            vmem((micro, height, breadth, channels), low),
            vmem((micro, tokens, channels), wide),
            vmem((micro, tokens, LANES), wide),
            vmem((micro, tokens, hidden_units), wide),
            vmem((micro, tokens, channels), wide),
            vmem((micro, height, breadth, channels), low),
            vmem((micro, tall, breadth, channels), low),
            vmem((micro, height, breadth, channels), low),
            vmem((micro, height, breadth, channels), low),
            vmem((height, breadth, channels), wide),
            vmem((height, breadth, channels), wide),
            vmem((tokens, channels), wide),
            vmem((tall, breadth + 2 * SIDE, channels), wide),
            vmem((spots, 1, channels), wide),
            vmem((spots, 8, channels), wide),
            vmem((4, 8, channels), wide),
            vmem((slabs, share, channels), wide),
            vmem((slabs, share, channels), wide),
            vmem((slabs, share, channels), wide),
            dma((micro, 3)), dma((micro, 3)), dma((micro, 3)),
            dma((micro, 4)), dma((micro, 4)),
            dma, dma,
            dma((slabs,)), dma((slabs,)), dma((slabs,)), dma((slabs,)),
            dma((11,)), dma((2, slabs, 2 + copies)), dma((2, slabs, copies)),
        ],
        compiler_params=pltpu.CompilerParams(
            collective_id=0, has_side_effects=True, vmem_limit_bytes=62 * 1024 * 1024
        ),
        name="block_chain",
    )(
        latent, target, w_expand, expand_bias, w_reduce, reduce_bias,
        depth_kernel.transpose(1, 0, 2), depth_offset, norm_gain, norm_shift, layer_scale,
    )
    return (found[0].transpose(1, 0, 2),) + tuple(found[1:])


def solution(mesh):
    image = P("groups", "rows", None, None)
    matrix, vector = P("section", "rows", None), P("section", None)
    both = ("groups", "section")
    return jax.shard_map(
        per_device,
        mesh=mesh,
        in_specs=(
            image, image, matrix, vector, matrix, vector,
            P("section", None, None), vector, vector, vector, vector,
        ),
        out_specs=(P(both, None, None),) + (P(both, None),) * 4,
        check_vma=False,
    )
```
